32 devices in a mesh: rep: 8 (over y, x, core), dom: 4 (over z).
Axes of the slice: x: 2, y: 2, z: 4, core: 2. Of those that a mesh axis runs over, the one named last changes fastest.
Arguments:
- block_input: bfloat16 [32, 8, 16, 320], P(('rep', 'dom')), may hold values from -36 to 36
- cotangent: bfloat16 [32, 8, 16, 320], P(('rep', 'dom')), may hold values from -6 to 6
- timesteps: int32 [32], P(('rep', 'dom')), may hold values from 0 to 999
- owner_map: int32 [4], replicated, may hold values from 0 to 3, each once
- time_weight: bfloat16 [1280, 320], replicated, may hold values from -0.15625 to 0.15625
- first_weight: bfloat16 [2880, 320], P('dom'), may hold values from -0.109375 to 0.109375
- second_weight: bfloat16 [2880, 320], P('dom'), may hold values from -0.109375 to 0.109375
Outputs:
- block_output: bfloat16 [32, 8, 16, 320], P(('rep', 'dom'))
- first_grad: float32 [2880, 320], P('dom')
- second_grad: float32 [2880, 320], P('dom')
The draws below stay inside these ranges and needn't reach their ends.
Inputs may be any that keep to these rules, and one draw needn't show every extreme that they name: `owner_map`: each dom index holds exactly one block.
All inputs are finite; a program needn't handle non-finite values.
Results may differ from the reference program's by a relative error of at most 0.0064.
Values may be sent and summed in bfloat16 or wider, within the bound.
No kernel may reach another device: no remote copies, remote signals or barrier semaphores. Data moves between devices by JAX's collectives and lax.ppermute only.
A program may use at most 64 MiB of HBM per device.

```python
import math
import jax
import jax.numpy as jnp
from jax import lax

C = 320
GROUPS = 32
TEMB = 1280
HEIGHT = 8
WIDTH = 16
SAMPLES = 32
DOM_BLOCKS = 4
N_DOM = 4


def draw_block_input(key, part):
    first_key, second_key, third_key = jax.random.split(key, 3)
    shape_full = (SAMPLES, HEIGHT, WIDTH, C)
    standard = jnp.clip(jax.random.normal(first_key, shape_full, jnp.float32), -6.0, 6.0)
    pixel_scale = jnp.exp(jax.random.uniform(second_key, (SAMPLES, HEIGHT, WIDTH, 1), jnp.float32, math.log(0.3), math.log(3.0)))
    channel_scale = jnp.exp(jax.random.uniform(third_key, (1, 1, 1, C), jnp.float32, math.log(0.5), math.log(2.0)))
    return (standard * pixel_scale * channel_scale).astype(jnp.bfloat16)


def touch_ends(array, rng, smallest, largest):
    extent = array.shape
    place = [jax.random.randint(jax.random.fold_in(rng, axis), (), 0, extent[axis]) for axis in range(len(extent))]
    array = array.at[tuple(place)].set(smallest)
    longest = extent.index(max(extent))
    place[longest] = (place[longest] + 1) % extent[longest]
    return array.at[tuple(place)].set(largest)


def block_scale(own_key, dims, cuts, least, largest):
    factor_of, own = 1.0, jax.random.fold_in(own_key, 6)
    for position, parts in cuts:
        heights = jnp.exp(jax.random.uniform(jax.random.fold_in(own, position), (parts,), jnp.float32, least / len(cuts), largest / len(cuts)))
        factor_of = factor_of * jnp.repeat(heights, dims[position] // parts).reshape([-1 if axis == position else 1 for axis in range(len(dims))])
    return factor_of


def normal_values(key, dims, width, bound, cuts=(), held_as=jnp.bfloat16):
    values = jax.random.normal(key, dims, jnp.float32) * width
    if len(cuts) > 0:
        values = block_scale(key, dims, cuts, -0.22, 0.18) * values
    return jnp.clip(values, min=-bound, max=bound).astype(held_as)


def setup_inputs(seed: int = 0) -> dict:
    keys = jax.random.split(jax.random.key(seed), 8)
    block_input = draw_block_input(jax.random.fold_in(keys[7], 71), 0)
    cotangent = normal_values(keys[1], (SAMPLES, HEIGHT, WIDTH, C), 1.0, 6.0, ((0, 32),))
    timesteps = touch_ends(jax.random.randint(keys[2], (SAMPLES,), 0, 1000), jax.random.fold_in(keys[2], 1), 0, 999).astype(jnp.int32)
    owner_map = jax.random.permutation(keys[3], DOM_BLOCKS).astype(jnp.int32)
    time_weight = normal_values(keys[4], (TEMB, C), TEMB ** -0.5, 0.15625)
    first_weight = normal_values(keys[5], (9 * C, C), (9 * C) ** -0.5, 0.109375, ((0, 4),))
    second_weight = normal_values(keys[6], (9 * C, C), (9 * C) ** -0.5, 0.109375, ((0, 4),))
    return dict(block_input=block_input, cotangent=cotangent, timesteps=timesteps, owner_map=owner_map, time_weight=time_weight, first_weight=first_weight, second_weight=second_weight)


norm_eps = 1e-05

def columns(activation):
    padded = jnp.pad(activation, ((1, 1), (1, 1), (0, 0)))
    pieces = []
    for row_tap in range(3):
        for col_tap in range(3):
            pieces.append(padded[row_tap:row_tap + HEIGHT, col_tap:col_tap + WIDTH, :])
    return jnp.concatenate(pieces, axis=-1).reshape(HEIGHT * WIDTH, 9 * C)

def spread_back(gathered):
    framed = jnp.pad(gathered.reshape(HEIGHT, WIDTH, 9, C), ((1, 1), (1, 1), (0, 0), (0, 0)))
    result = jnp.zeros((HEIGHT, WIDTH, C), jnp.float32)
    for row_tap in range(3):
        for col_tap in range(3):
            result = result + framed[2 - row_tap:2 - row_tap + HEIGHT, 2 - col_tap:2 - col_tap + WIDTH, 3 * row_tap + col_tap, :]
    return result.reshape(HEIGHT * WIDTH, C)

def group_norm(values):
    grouped = values.reshape(HEIGHT * WIDTH, GROUPS, C // GROUPS)
    center = lax.optimization_barrier(jnp.mean(grouped, axis=(0, 2), keepdims=True))
    spread = lax.optimization_barrier(jnp.mean(jnp.square(grouped - center), axis=(0, 2), keepdims=True))
    inverse_std = lax.rsqrt(spread + norm_eps)
    return (((grouped - center) * inverse_std).reshape(HEIGHT * WIDTH, C), inverse_std)

def norm_back(incoming, normed, inverse_std):
    grouped_grad = incoming.reshape(HEIGHT * WIDTH, GROUPS, C // GROUPS)
    grouped_norm = normed.reshape(HEIGHT * WIDTH, GROUPS, C // GROUPS)
    mean_grad = lax.optimization_barrier(jnp.mean(grouped_grad, axis=(0, 2), keepdims=True))
    mean_prod = lax.optimization_barrier(jnp.mean(grouped_grad * grouped_norm, axis=(0, 2), keepdims=True))
    return (inverse_std * (grouped_grad - mean_grad - grouped_norm * mean_prod)).reshape(HEIGHT * WIDTH, C)

def time_bias(timestep, time_weight):
    half_dim = TEMB // 2
    frequency = jnp.exp(-math.log(10000.0) * jnp.arange(half_dim, dtype=jnp.float32) / half_dim)
    angles = timestep.astype(jnp.float32) * frequency
    embedded = jnp.concatenate([jnp.cos(angles), jnp.sin(angles)])
    activated = jax.nn.silu(embedded).astype(jnp.bfloat16)
    return jnp.dot(activated[None, :], time_weight, preferred_element_type=jnp.float32)

def logical(stored, owner_map):
    blocks = stored.reshape(N_DOM, 9 * C // N_DOM, C)
    return jnp.take(blocks, owner_map, axis=0).reshape(9 * C, C)

def to_stored(logical_grad, owner_map):
    blocks = logical_grad.reshape(N_DOM, 9 * C // N_DOM, C)
    return jnp.zeros_like(blocks).at[owner_map].set(blocks).reshape(9 * C, C)

def round_term(product):
    return lax.optimization_barrier(product.astype(jnp.bfloat16)).astype(jnp.float32)

def sample_pass(inputs_one, cotangent_one, timestep, time_weight, first_logic, second_logic):
    source = inputs_one.astype(jnp.float32).reshape(HEIGHT * WIDTH, C)
    normed, unused_std = group_norm(source)
    first_act = jax.nn.silu(normed).astype(jnp.bfloat16)
    first_cols = columns(first_act.reshape(HEIGHT, WIDTH, C))
    first_conv = jnp.dot(first_cols, first_logic, preferred_element_type=jnp.float32) + time_bias(timestep, time_weight)
    second_norm, second_std = group_norm(first_conv)
    second_act = jax.nn.silu(second_norm).astype(jnp.bfloat16)
    second_cols = columns(second_act.reshape(HEIGHT, WIDTH, C))
    output = (source + jnp.dot(second_cols, second_logic, preferred_element_type=jnp.float32)).astype(jnp.bfloat16)
    upstream = cotangent_one.reshape(HEIGHT * WIDTH, C)
    second_term = round_term(lax.dot_general(second_cols, upstream, (((0,), (0,)), ((), ())), preferred_element_type=jnp.float32))
    second_back = lax.dot_general(upstream, second_logic, (((1,), (1,)), ((), ())), preferred_element_type=jnp.float32)
    act_grad = spread_back(second_back)
    gate_value = jax.nn.sigmoid(second_norm)
    norm_grad = act_grad * gate_value * (1.0 + second_norm * (1.0 - gate_value))
    conv_grad = norm_back(norm_grad, second_norm, second_std).astype(jnp.bfloat16)
    first_term = round_term(lax.dot_general(first_cols, conv_grad, (((0,), (0,)), ((), ())), preferred_element_type=jnp.float32))
    return (output.reshape(HEIGHT, WIDTH, C), first_term, second_term)

def reference(block_input, cotangent, timesteps, owner_map, time_weight, first_weight, second_weight):
    first_logic = logical(first_weight, owner_map)
    second_logic = logical(second_weight, owner_map)

    def accumulate(totals, packed):
        inputs_one, cotangent_one, timestep = packed
        output, first_term, second_term = sample_pass(inputs_one, cotangent_one, timestep, time_weight, first_logic, second_logic)
        return ((totals[0] + first_term, totals[1] + second_term), output)
    zero_grad = jnp.zeros((9 * C, C), jnp.float32)
    totals, outputs = lax.scan(accumulate, (zero_grad, zero_grad), (block_input, cotangent, timesteps))
    first_grad = to_stored(totals[0] / SAMPLES, owner_map)
    second_grad = to_stored(totals[1] / SAMPLES, owner_map)
    return (outputs, first_grad, second_grad)
```

```python
import functools
import math

import jax
import jax.numpy as jnp
from jax import lax
from jax.experimental import pallas as pl
from jax.experimental.pallas import tpu as pltpu
from jax.sharding import PartitionSpec as P

GROUPS = 32
NORM_EPS = 1e-05
F32 = jnp.float32
BF16 = jnp.bfloat16
HIGHEST = lax.Precision.HIGHEST


def round_up(value, unit):
    return -(-value // unit) * unit


def nn(a, b, precision=None):
    return lax.dot_general(
        a, b, (((1,), (0,)), ((), ())), precision=precision, preferred_element_type=F32
    )


def nt(a, b):
    return lax.dot_general(a, b, (((1,), (1,)), ((), ())), preferred_element_type=F32)


def tn(a, b):
    return lax.dot_general(a, b, (((0,), (0,)), ((), ())), preferred_element_type=F32)


def iota(shape, axis):
    return lax.broadcasted_iota(jnp.int32, shape, axis)


def quotient(value, unit):
    return jnp.floor((value.astype(F32) + 0.5) * (1.0 / unit)).astype(jnp.int32)


def one_hot(hit):
    return jnp.where(hit, 1.0, 0.0).astype(BF16)


def silu(value):
    return value / (1.0 + jnp.exp(-value))


class Plan:
    def __init__(self, n_rep, n_dom, height, width, channels, embed, block_rows):
        self.n_rep, self.n_dom = n_rep, n_dom
        self.height, self.width, self.channels = height, width, channels
        self.embed, self.block_rows = embed, block_rows
        self.pixels = height * width
        self.per_group = channels // GROUPS
        team = 1
        while (
            n_rep % (2 * team) == 0
            and GROUPS % (2 * team) == 0
            and block_rows % (2 * team * self.per_group) == 0
        ):
            team *= 2
        self.team = team
        self.local = channels // team
        self.stretch = self.per_group * team
        self.stretches = block_rows // self.stretch
        self.quarters = channels // self.stretch
        self.piece = self.stretches * self.per_group
        self.piece_pad = round_up(self.piece, 16)
        self.wide = round_up(3 * self.local, 128)
        self.act_rows = self.pixels + 16

    def dom_peer(self, here, step):
        if self.n_dom & (self.n_dom - 1) == 0:
            return here ^ step
        return lax.rem(here + step, self.n_dom)

    def dom_source(self, here, step):
        if self.n_dom & (self.n_dom - 1) == 0:
            return here ^ step
        return lax.rem(here - step + self.n_dom, self.n_dom)


def logical_of(plan, owner_ref, holder):
    total = 0
    for block in range(plan.n_dom):
        total = total + jnp.where(owner_ref[block] == holder, block, 0)
    return total


def group_matrix(plan, lanes, channels):
    row, col = iota((lanes, lanes), 0), iota((lanes, lanes), 1)
    same = quotient(row, plan.per_group) == quotient(col, plan.per_group)
    return jnp.where(same & (row < channels) & (col < channels), 1.0, 0.0)


def prep_kernel(plan, place_ref, steps_ref, x_ref, tw_ref, w1_ref, w2_ref, act_ref, s1_ref, s2_ref):
    c, pix = plan.channels, plan.pixels
    spot = place_ref[0]
    row, col = iota((plan.local, c), 0), iota((plan.local, c), 1)
    band = quotient(row, plan.per_group)
    wanted = band * plan.stretch + spot * plan.per_group + row - band * plan.per_group
    s1_ref[...] = nn(one_hot(col == wanted), w1_ref[...]).astype(BF16)
    row, col = iota((plan.piece_pad, plan.block_rows), 0), iota((plan.piece_pad, plan.block_rows), 1)
    band = quotient(row, plan.per_group)
    wanted = band * plan.stretch + spot * plan.per_group + row - band * plan.per_group
    s2_ref[...] = nt(one_hot((col == wanted) & (row < plan.piece)), w2_ref[...]).astype(BF16)
    x = x_ref[...].astype(F32)
    same = group_matrix(plan, c, c)
    count = pix * plan.per_group
    center = nn(jnp.broadcast_to(jnp.sum(x, 0, keepdims=True), (8, c)), same, HIGHEST)[0:1] / count
    off = x - center
    spread = nn(jnp.broadcast_to(jnp.sum(off * off, 0, keepdims=True), (8, c)), same, HIGHEST)[0:1] / count
    act_ref[0:pix, :] = silu(off * lax.rsqrt(spread + NORM_EPS)).astype(BF16)
    half = plan.embed // 2
    lane = iota((8, plan.embed), 1)
    k = jnp.where(lane < half, lane, lane - half).astype(F32)
    angle = steps_ref[0].astype(F32) * jnp.exp(-math.log(10000.0) * k / half)
    wave = jnp.where(lane < half, jnp.cos(angle), jnp.sin(angle))
    bias = nt(silu(wave).astype(BF16), tw_ref[...])
    high = bias.astype(BF16)
    rest = bias - high.astype(F32)
    mid = rest.astype(BF16)
    low = (rest - mid.astype(F32)).astype(BF16)
    which = iota((16, c), 0)
    high, mid, low = (jnp.concatenate([v.astype(F32)] * 2, axis=0) for v in (high, mid, low))
    tail = jnp.where(which == 0, high, jnp.where(which == 1, mid, jnp.where(which == 2, low, 0.0)))
    act_ref[pix:, :] = tail.astype(BF16)


def roll_rows(value, shift, width, plan):
    rows = value.shape[0]
    moved = pltpu.roll(value, shift % rows, 0)
    x = iota(value.shape, 0) & (width - 1) if width & (width - 1) == 0 else lax.rem(iota(value.shape, 0), width)
    return jnp.where(x == (0 if shift == 1 else width - 1), 0.0, moved)


def roll_lanes(value, shift):
    lanes = value.shape[1]
    return value if shift % lanes == 0 else pltpu.roll(value, shift % lanes, 1)


def gather_taps(wide, plan, sign):
    left = roll_rows(wide, sign, plan.width, plan)
    right = roll_rows(roll_lanes(wide, -2 * plan.local), -sign, plan.width, plan)
    return left + roll_lanes(wide, -plan.local) + right


def spread_taps(value, plan, sign):
    left = roll_rows(value, sign, plan.width, plan)
    right = roll_rows(value, -sign, plan.width, plan)
    return left + roll_lanes(value, plan.local) + roll_lanes(right, 2 * plan.local)


def main_kernel(plan, n_team, *refs):
    d, c, pix, local, wide = plan.n_dom, plan.channels, plan.pixels, plan.local, plan.wide
    place_ref, owner_ref = refs[0:2]
    acts = refs[2 : 2 + n_team]
    cots = refs[2 + n_team : 2 + 2 * n_team]
    w1s = refs[2 + 2 * n_team : 2 + 2 * n_team + d]
    w2s = refs[2 + 2 * n_team + d : 2 + 2 * n_team + 2 * d]
    rest = refs[2 + 2 * n_team + 2 * d :]
    part_ref = rest[0]
    g1s = rest[1 : 1 + d]
    g2s = rest[1 + d : 1 + 2 * d]
    actp, cotp, act2p, w1st, w2st, g1st = rest[1 + 2 * d :]
    spot, here = place_ref[0], place_ref[1]
    rows = n_team * pix
    width = plan.width

    for pad in (actp, cotp):
        pad[:, 0:width, :] = jnp.zeros((n_team, width, c), BF16)
        pad[:, width + pix :, :] = jnp.zeros((n_team, width, c), BF16)
    act2p[:, 0:width, :] = jnp.zeros((n_team, width, wide), BF16)
    act2p[:, width + pix :, :] = jnp.zeros((n_team, width, wide), BF16)
    for slot in range(n_team):
        actp[slot, width : width + pix, :] = acts[slot][0:pix, :]
        cotp[slot, width : width + pix, :] = cots[slot][...]

    def window(pad, tap):
        return pad[:, tap * width : tap * width + pix, :].reshape(rows, pad.shape[2])

    for slot in range(d):
        block = logical_of(plan, owner_ref, plan.dom_source(here, slot))
        w1st[block] = w1s[slot][...].astype(F32)
        w2st[slot] = w2s[slot][...]
    flat = jnp.concatenate([w1st[b] for b in range(d)], axis=1)
    zeros = [jnp.zeros((wide - 3 * local, c), F32)] if wide > 3 * local else []
    w1k = [
        jnp.concatenate(
            [flat[:, (3 * ky + kx) * c : (3 * ky + kx + 1) * c] for kx in range(3)] + zeros, axis=0
        ).astype(BF16)
        for ky in range(3)
    ]
    row, col = iota((3 * wide, plan.piece_pad), 0), iota((3 * wide, plan.piece_pad), 1)
    band = quotient(row, wide)
    within = row - band * wide
    compact = jnp.where(within < 3 * local, band * 3 * local + within, -1)
    w2all = jnp.zeros((3 * wide, c), F32)
    for slot in range(d):
        block = logical_of(plan, owner_ref, plan.dom_source(here, slot))
        hit = (col < plan.piece) & (compact == block * plan.piece + col)
        w2all = w2all + nn(one_hot(hit), w2st[slot])
    w2k = [w2all[ky * wide : (ky + 1) * wide].astype(BF16) for ky in range(3)]

    total = jnp.zeros((rows, wide), F32)
    for ky in range(3):
        total = total + nt(window(actp, ky), w1k[ky])
    conv = gather_taps(total, plan, 1)
    row, col = iota((c, wide), 0), iota((c, wide), 1)
    band = quotient(col, plan.per_group)
    wanted = band * plan.stretch + spot * plan.per_group + col - band * plan.per_group
    pick = one_hot((col < local) & (row == wanted))
    lane_ok = iota((1, wide), 1) < local
    same = group_matrix(plan, wide, local)
    count = pix * plan.per_group

    def group_mean(value):
        sums = jnp.sum(value.reshape(n_team, pix, wide), axis=1)
        if n_team < 8:
            sums = jnp.concatenate([sums, jnp.zeros((8 - n_team, wide), F32)], axis=0)
        return nn(sums, same, HIGHEST)[0:n_team].reshape(n_team, 1, wide) / count

    biases = []
    for slot in range(n_team):
        split = nn(acts[slot][pix:, :], pick)
        biases.append(split[0:1] + split[1:2] + split[2:3])
    bias = jnp.concatenate(biases, axis=0).reshape(n_team, 1, wide)
    conv = jnp.where(lane_ok, conv, 0.0).reshape(n_team, pix, wide) + bias
    off = conv - group_mean(conv.reshape(rows, wide))
    inverse = lax.rsqrt(group_mean((off * off).reshape(rows, wide)) + NORM_EPS)
    norm = off * inverse
    gate = 1.0 / (1.0 + jnp.exp(-norm))
    act2 = norm * gate
    act2x = spread_taps(act2.reshape(rows, wide), plan, 1)
    act2p[:, width : width + pix, :] = act2x.astype(BF16).reshape(n_team, pix, wide)

    out = jnp.zeros((rows, c), F32)
    for ky in range(3):
        out = out + nn(window(act2p, ky), w2k[ky])
    part_ref[...] = out.astype(BF16).reshape(n_team, pix, c)

    act2t = act2x.T.astype(BF16)
    second = jnp.concatenate([nn(act2t, window(cotp, 2 - ky)) for ky in range(3)], axis=0).astype(BF16)
    row, col = iota((plan.piece_pad, 3 * wide), 0), iota((plan.piece_pad, 3 * wide), 1)
    band = quotient(col, wide)
    within = col - band * wide
    compact = jnp.where(within < 3 * local, band * 3 * local + within, -1)
    for slot in range(d):
        block = logical_of(plan, owner_ref, plan.dom_peer(here, slot))
        hit = (row < plan.piece) & (compact == block * plan.piece + row)
        g2s[slot][...] = nn(one_hot(hit), second).astype(BF16)

    back = jnp.zeros((rows, wide), F32)
    for ky in range(3):
        back = back + nt(window(cotp, 2 - ky), w2k[ky])
    back = jnp.where(lane_ok, gather_taps(back, plan, -1), 0.0).reshape(n_team, pix, wide)
    grad = back * gate * (1.0 + norm * (1.0 - gate))
    grad_mean = group_mean(grad.reshape(rows, wide))
    prod_mean = group_mean((grad * norm).reshape(rows, wide))
    grad = inverse * (grad - grad_mean - norm * prod_mean)
    grad = jnp.where(lane_ok, grad, 0.0).reshape(rows, wide)

    gradt = spread_taps(grad.astype(BF16).astype(F32), plan, -1).T.astype(BF16)
    parts = [nn(gradt, window(actp, ky)) for ky in range(3)]
    flat = jnp.concatenate(
        [parts[t // 3][(t % 3) * local : (t % 3 + 1) * local] for t in range(9)], axis=1
    )
    for block in range(d):
        g1st[block] = flat[:, block * plan.block_rows : (block + 1) * plan.block_rows]
    for slot in range(d):
        block = logical_of(plan, owner_ref, plan.dom_peer(here, slot))
        g1s[slot][...] = g1st[block].astype(BF16)


def sum_kernel(n, *refs):
    outs = refs[-len(refs) // (n + 1) :]
    for i, out in enumerate(outs):
        total = refs[i][...].astype(F32)
        for k in range(1, n):
            total = total + refs[i + k * len(outs)][...].astype(F32)
        out[...] = total.astype(out.dtype)


def pair_kernel(n, part_ref, came_ref, out_ref):
    for k in range(n):
        out_ref[k] = (part_ref[2 * k].astype(F32) + came_ref[k].astype(F32)).astype(BF16)


def out_kernel(n, *refs):
    total = refs[0][...].astype(F32)
    for k in range(1, n + 1):
        total = total + refs[k][...].astype(F32)
    refs[n + 1][...] = total.astype(BF16)


def last_kernel(plan, n_team, scale, place_ref, *refs):
    local, c, r = plan.local, plan.channels, plan.block_rows
    firsts, seconds = refs[0:n_team], refs[n_team : 2 * n_team]
    out1, out2, st1, st2 = refs[2 * n_team :]
    spot = place_ref[0]
    for slot in range(n_team):
        st1[spot ^ slot] = firsts[slot][...].astype(F32)
        st2[spot ^ slot] = seconds[slot][...]
    row, col = iota((c, n_team * local), 0), iota((c, n_team * local), 1)
    who = quotient(col, local)
    inner = col - who * local
    band = quotient(inner, plan.per_group)
    wanted = band * plan.stretch + who * plan.per_group + inner - band * plan.per_group
    stacked = st1[...].reshape(n_team * local, r).astype(BF16)
    out1[...] = nn(one_hot(row == wanted), stacked) * scale
    row, col = iota((n_team * plan.piece_pad, r), 0), iota((n_team * plan.piece_pad, r), 1)
    who = quotient(row, plan.piece_pad)
    inner = row - who * plan.piece_pad
    band = quotient(inner, plan.per_group)
    wanted = band * plan.stretch + who * plan.per_group + inner - band * plan.per_group
    stacked = st2[...].reshape(n_team * plan.piece_pad, c)
    out2[...] = tn(stacked, one_hot((inner < plan.piece) & (col == wanted))) * scale


VMEM = pl.BlockSpec(memory_space=pltpu.VMEM)
SMEM = pl.BlockSpec(memory_space=pltpu.SMEM)


def call(kernel, name, out_shape, operands, n_smem=0, scratch=()):
    n = len(operands)
    return pl.pallas_call(
        kernel,
        name=name,
        out_shape=out_shape,
        in_specs=[SMEM] * n_smem + [VMEM] * (n - n_smem),
        out_specs=jax.tree.map(lambda _: VMEM, out_shape),
        scratch_shapes=list(scratch),
        compiler_params=pltpu.CompilerParams(vmem_limit_bytes=48 * 1024 * 1024),
    )(*operands)


def shape(dims, dtype):
    return jax.ShapeDtypeStruct(dims, dtype)


def body(block_input, cotangent, timesteps, owner_map, time_weight, first_weight, second_weight):
    n_rep, n_dom = lax.axis_size("rep"), lax.axis_size("dom")
    height, width, c = block_input.shape[1:]
    plan = Plan(n_rep, n_dom, height, width, c, time_weight.shape[0], first_weight.shape[0])
    team, d, pix = plan.team, n_dom, plan.pixels
    r, local = plan.block_rows, plan.local
    here = lax.axis_index("dom")
    spot = lax.axis_index("rep") % team
    place = jnp.stack([spot, here]).astype(jnp.int32)

    def to_rep(value, step):
        return lax.ppermute(value, "rep", [(i, i ^ step) for i in range(n_rep)])

    def to_dom(value, step):
        if d & (d - 1) == 0:
            return lax.ppermute(value, "dom", [(i, i ^ step) for i in range(d)])
        return lax.ppermute(value, "dom", [(i, (i + step) % d) for i in range(d)])

    def team_gather(value):
        slots = [value] + [None] * (team - 1)
        for step in reversed(range(2, team, 2)):
            slots[step] = to_rep(value, step)
        if team > 1:
            for step in range(0, team, 2):
                slots[step + 1] = to_rep(slots[step], 1)
        return slots

    def dom_gather(value):
        return [value] + [to_dom(value, step) for step in range(1, d)]

    x = block_input.reshape(pix, c)
    cot = cotangent.reshape(pix, c)
    act, s1, s2 = call(
        functools.partial(prep_kernel, plan),
        "prep",
        (
            shape((plan.act_rows, c), BF16),
            shape((local, r), BF16),
            shape((plan.piece_pad, c), BF16),
        ),
        (place, timesteps, x, time_weight.T, first_weight.T, second_weight.T),
        n_smem=2,
    )
    w1s, w2s = dom_gather(s1), dom_gather(s2)
    acts, cots = team_gather(act), team_gather(cot)
    rows = (height + 2) * width
    outs = call(
        functools.partial(main_kernel, plan, team),
        "main",
        (
            shape((team, pix, c), BF16),
            *[shape((local, r), BF16)] * d,
            *[shape((plan.piece_pad, c), BF16)] * d,
        ),
        (place, owner_map, *acts, *cots, *w1s, *w2s),
        n_smem=2,
        scratch=(
            pltpu.VMEM((team, rows, c), BF16),
            pltpu.VMEM((team, rows, c), BF16),
            pltpu.VMEM((team, rows, plan.wide), BF16),
            pltpu.VMEM((d, local, r), F32),
            pltpu.VMEM((d, plan.piece_pad, c), BF16),
            pltpu.VMEM((d, local, r), F32),
        ),
    )
    part, g1s, g2s = outs[0], outs[1 : 1 + d], outs[1 + d :]

    got1 = [g1s[0]] + [to_dom(g1s[k], k) for k in range(1, d)]
    got2 = [g2s[0]] + [to_dom(g2s[k], k) for k in range(1, d)]
    mine = BF16 if n_rep == team else F32
    sum1, sum2 = call(
        functools.partial(sum_kernel, d),
        "owner_sum",
        (shape((local, r), mine), shape((plan.piece_pad, c), mine)),
        tuple(v for pair in zip(got1, got2) for v in pair),
    )
    if n_rep > team:
        same_spot = [[i * team + k for i in range(n_rep // team)] for k in range(team)]
        sum1, sum2 = lax.psum((sum1, sum2), "rep", axis_index_groups=same_spot)
        sum1, sum2 = sum1.astype(BF16), sum2.astype(BF16)
    firsts, seconds = team_gather(sum1), team_gather(sum2)
    first, second = call(
        functools.partial(last_kernel, plan, team, 1.0 / (n_rep * n_dom)),
        "assemble",
        (shape((c, r), F32), shape((c, r), F32)),
        (place, *firsts, *seconds),
        n_smem=1,
        scratch=(
            pltpu.VMEM((team, local, r), F32),
            pltpu.VMEM((team, plan.piece_pad, c), BF16),
        ),
    )

    if team > 1:
        away = part.reshape(team // 2, 2, pix, c)[:, 1]
        half = call(
            functools.partial(pair_kernel, team // 2),
            "pair_sum",
            shape((team // 2, pix, c), BF16),
            (part, to_rep(away, 1)),
        )
        shares = [half[0]] + [to_rep(half[k], 2 * k) for k in range(1, team // 2)]
    else:
        shares = [part[0]]
    output = call(
        functools.partial(out_kernel, len(shares)), "output", shape((pix, c), BF16), (x, *shares)
    )
    return output.reshape(1, height, width, c), first.T, second.T


def solution(mesh):
    placed = (
        P(("rep", "dom"), None, None, None),
        P(("rep", "dom"), None, None, None),
        P(("rep", "dom")),
        P(),
        P(),
        P("dom", None),
        P("dom", None),
    )
    return jax.shard_map(
        body,
        mesh=mesh,
        in_specs=placed,
        out_specs=(P(("rep", "dom"), None, None, None), P("dom", None), P("dom", None)),
        check_vma=False,
    )
```

```python
import functools
import math

import jax
import jax.numpy as jnp
from jax import lax
from jax.experimental import pallas as pl
from jax.experimental.pallas import tpu as pltpu
from jax.sharding import PartitionSpec as P

GROUPS = 32
NORM_EPS = 1e-05
F32 = jnp.float32
BF16 = jnp.bfloat16
HIGHEST = lax.Precision.HIGHEST


def round_up(value, unit):
    return -(-value // unit) * unit


def nn(a, b, precision=None):
    return lax.dot_general(
        a, b, (((1,), (0,)), ((), ())), precision=precision, preferred_element_type=F32
    )


def nt(a, b):
    return lax.dot_general(a, b, (((1,), (1,)), ((), ())), preferred_element_type=F32)


def tn(a, b):
    return lax.dot_general(a, b, (((0,), (0,)), ((), ())), preferred_element_type=F32)


def iota(shape, axis):
    return lax.broadcasted_iota(jnp.int32, shape, axis)


def quotient(value, unit):
    return jnp.floor((value.astype(F32) + 0.5) * (1.0 / unit)).astype(jnp.int32)


def one_hot(hit):
    return jnp.where(hit, 1.0, 0.0).astype(BF16)


def silu(value):
    return value / (1.0 + jnp.exp(-value))


class Plan:
    def __init__(self, n_rep, n_dom, height, width, channels, embed, block_rows):
        if n_dom < 2 or n_dom & (n_dom - 1):
            raise ValueError("dom size")
        self.n_rep, self.n_dom = n_rep, n_dom
        self.height, self.width, self.channels = height, width, channels
        self.embed, self.block_rows = embed, block_rows
        self.pixels = height * width
        self.per_group = channels // GROUPS
        team = 1
        while (
            n_rep % (2 * team) == 0
            and GROUPS % (2 * team) == 0
            and block_rows % (2 * team * self.per_group) == 0
        ):
            team *= 2
        self.team = team
        self.local = channels // team
        self.stretch = self.per_group * team
        self.stretches = block_rows // self.stretch
        self.quarters = channels // self.stretch
        self.piece = self.stretches * self.per_group
        self.piece_pad = round_up(self.piece, 16)
        self.wide = round_up(3 * self.local, 128)
        self.act_rows = self.pixels + 16
        self.head = channels // 128 * 128
        self.packed = 2 * channels
        more = block_rows - self.packed
        if more > 0:
            self.first_rows = self.local + folded_rows(self, self.local, more)
        else:
            self.first_rows = folded_rows(self, self.local, block_rows)
        self.first_rows = round_up(self.first_rows, 16)
        self.second_rows = round_up(folded_rows(self, self.piece_pad, channels), 16)


def own_spot(plan):
    return lax.rem(lax.axis_index("rep"), plan.team)


def logical_of(plan, owner_ref, holder):
    total = 0
    for block in range(plan.n_dom):
        total = total + jnp.where(owner_ref[block] == holder, block, 0)
    return total


def group_matrix(plan, lanes, channels):
    row, col = iota((lanes, lanes), 0), iota((lanes, lanes), 1)
    same = quotient(row, plan.per_group) == quotient(col, plan.per_group)
    return jnp.where(same & (row < channels) & (col < channels), 1.0, 0.0)


def fold(plan, value):
    rows, lanes = value.shape
    fits = plan.packed // lanes
    chunk = round_up(-(-rows // fits), 8)
    if chunk * fits > rows:
        value = jnp.concatenate([value, jnp.zeros((chunk * fits - rows, lanes), F32)], axis=0)
    parts = [value[i * chunk : (i + 1) * chunk] for i in range(fits)]
    if fits * lanes < plan.packed:
        parts.append(jnp.zeros((chunk, plan.packed - fits * lanes), F32))
    return parts[0] if len(parts) == 1 else jnp.concatenate(parts, axis=1)


def unfold(plan, value, rows, lanes):
    fits = plan.packed // lanes
    parts = [value[:, i * lanes : (i + 1) * lanes] for i in range(fits)]
    return jnp.concatenate(parts, axis=0)[0:rows]


def folded_rows(plan, rows, lanes):
    return round_up(-(-rows // (plan.packed // lanes)), 8)


def pack_first(plan, value):
    if plan.block_rows > plan.packed:
        parts = [value[:, 0 : plan.packed], fold(plan, value[:, plan.packed :])]
    else:
        parts = [fold(plan, value)]
    have = sum(part.shape[0] for part in parts)
    if have < plan.first_rows:
        parts.append(jnp.zeros((plan.first_rows - have, plan.packed), F32))
    return jnp.concatenate(parts, axis=0) if len(parts) > 1 else parts[0]


def unpack_first(plan, value):
    local, r = plan.local, plan.block_rows
    if r > plan.packed:
        more = r - plan.packed
        tail = unfold(plan, value[local : local + folded_rows(plan, local, more)], local, more)
        return jnp.concatenate([value[0:local], tail], axis=1)
    return unfold(plan, value[0 : folded_rows(plan, local, r)], local, r)


def pack_second(plan, value):
    value = fold(plan, value)
    if value.shape[0] < plan.second_rows:
        rest = jnp.zeros((plan.second_rows - value.shape[0], plan.packed), F32)
        value = jnp.concatenate([value, rest], axis=0)
    return value


def unpack_second(plan, value):
    rows = folded_rows(plan, plan.piece_pad, plan.channels)
    return unfold(plan, value[0:rows], plan.piece_pad, plan.channels)


def local_to_global(plan, index, spot):
    band = quotient(index, plan.per_group)
    return band * plan.stretch + spot * plan.per_group + index - band * plan.per_group


def slice_kernel(plan, w1_any, w2_any, pay_ref, w1_ref, w2_ref, sems):
    copies = [
        pltpu.make_async_copy(src, dst, sems.at[i])
        for i, (src, dst) in enumerate(((w1_any, w1_ref), (w2_any, w2_ref)))
    ]
    for copy in copies:
        copy.start()
    spot = own_spot(plan)
    row, col = iota((plan.local, plan.channels), 0), iota((plan.local, plan.channels), 1)
    pick1 = one_hot(col == local_to_global(plan, row, spot))
    row, col = iota((plan.piece_pad, plan.block_rows), 0), iota((plan.piece_pad, plan.block_rows), 1)
    pick2 = one_hot((col == local_to_global(plan, row, spot)) & (row < plan.piece))
    copies[0].wait()
    pay_ref[0 : plan.first_rows, :] = pack_first(plan, nn(pick1, w1_ref[...])).astype(BF16)
    copies[1].wait()
    pay_ref[plan.first_rows :, :] = pack_second(plan, nt(pick2, w2_ref[...])).astype(BF16)


def act_kernel(plan, steps_ref, x_any, cot_any, after_ref, act_ref, x_ref, cot_ref, sems):
    del after_ref
    copies = [
        pltpu.make_async_copy(x_any, x_ref, sems.at[0]),
        pltpu.make_async_copy(cot_any, cot_ref, sems.at[1]),
    ]
    for copy in copies:
        copy.start()
    c, pix, head = plan.channels, plan.pixels, plan.head
    half = plan.embed // 2
    k = iota((16, c), 0) * c + iota((16, c), 1)
    angle = jnp.where(k < half, k, k - half).astype(F32)
    angle = steps_ref[0].astype(F32) * jnp.exp(-math.log(10000.0) * angle / half)
    wave = silu(jnp.where(k < half, jnp.cos(angle), jnp.sin(angle)))
    wave = jnp.where(iota((16, c), 0) < plan.embed // c, wave, 0.0)
    act_ref[pix:, :] = jnp.concatenate([wave, jnp.zeros((16, c), F32)], axis=1).astype(BF16)
    same = group_matrix(plan, c, c)
    count = pix * plan.per_group
    copies[0].wait()
    x = x_ref[...].astype(F32)
    center = nn(jnp.broadcast_to(jnp.sum(x, 0, keepdims=True), (8, c)), same, HIGHEST)[0:1] / count
    off = x - center
    spread = nn(jnp.broadcast_to(jnp.sum(off * off, 0, keepdims=True), (8, c)), same, HIGHEST)[0:1] / count
    act = silu(off * lax.rsqrt(spread + NORM_EPS)).astype(BF16)
    copies[1].wait()
    act_ref[0:pix, 0:head] = act[:, 0:head]
    act_ref[0:pix, head : 2 * head] = cot_ref[:, 0:head]
    act_ref[0:pix, 2 * head :] = jnp.concatenate(
        [act[:, head:].astype(F32), cot_ref[:, head:].astype(F32)], axis=1
    ).astype(BF16)


def relay_kernel(pass_ref, *refs):
    refs[-1][...] = pass_ref[...]


def time_kernel(plan, tw_ref, out_ref, table1_ref, table2_ref):
    team = plan.team
    c = plan.channels
    row, col = iota((plan.wide, c), 0), iota((plan.wide, c), 1)
    pick = one_hot((row < plan.local) & (col == local_to_global(plan, row, own_spot(plan))))
    own = nn(pick, tw_ref[...])
    for part in range(plan.embed // c):
        out_ref[part] = own[:, part * c : (part + 1) * c].astype(BF16)
    row, col = iota((c, team * plan.local), 0), iota((c, team * plan.local), 1)
    who = quotient(col, plan.local)
    table1_ref[...] = one_hot(row == local_to_global(plan, col - who * plan.local, who))
    row, col = iota(table2_ref.shape, 0), iota(table2_ref.shape, 1)
    who = quotient(row, plan.piece_pad)
    inner = row - who * plan.piece_pad
    table2_ref[...] = one_hot((inner < plan.piece) & (col == local_to_global(plan, inner, who)))


def roll_rows(value, shift, width, plan):
    rows = value.shape[0]
    moved = pltpu.roll(value, shift % rows, 0)
    x = iota(value.shape, 0) & (width - 1) if width & (width - 1) == 0 else lax.rem(iota(value.shape, 0), width)
    return jnp.where(x == (0 if shift == 1 else width - 1), 0.0, moved)


def roll_lanes(value, shift):
    lanes = value.shape[1]
    return value if shift % lanes == 0 else pltpu.roll(value, shift % lanes, 1)


def gather_taps(wide, plan, sign):
    left = roll_rows(wide, sign, plan.width, plan)
    right = roll_rows(roll_lanes(wide, -2 * plan.local), -sign, plan.width, plan)
    return left + roll_lanes(wide, -plan.local) + right


def spread_taps(value, plan, sign):
    left = roll_rows(value, sign, plan.width, plan)
    right = roll_rows(value, -sign, plan.width, plan)
    return left + roll_lanes(value, plan.local) + roll_lanes(right, 2 * plan.local)


def window(plan, pad, tap):
    value = pad[:, tap * plan.width : tap * plan.width + plan.pixels, :]
    return value.reshape(value.shape[0] * plan.pixels, value.shape[2])


def fill_pad(plan, pad):
    pad[:, 0 : plan.width, :] = jnp.zeros((pad.shape[0], plan.width, pad.shape[2]), BF16)
    pad[:, plan.width + plan.pixels :, :] = jnp.zeros((pad.shape[0], plan.width, pad.shape[2]), BF16)


def group_mean(plan, value, same):
    team, wide = plan.team, plan.wide
    sums = jnp.sum(value.reshape(team, plan.pixels, wide), axis=1)
    if team < 8:
        sums = jnp.concatenate([sums, jnp.zeros((8 - team, wide), F32)], axis=0)
    return nn(sums, same, HIGHEST)[0:team].reshape(team, 1, wide) / (plan.pixels * plan.per_group)


def main_kernel(plan, owner_ref, *refs):
    team, d, c, pix, local, wide = plan.team, plan.n_dom, plan.channels, plan.pixels, plan.local, plan.wide
    pays, slices, tw_ref = refs[0:team], refs[team : team + d], refs[team + d]
    refs = refs[1:]
    act2p, w2_ref = refs[team + d : team + d + 2]
    pieces = refs[team + d + 2 : team + 2 * d + 2]
    actp, cotp, w1st, w2st, held = refs[team + 2 * d + 2 :]
    here = lax.axis_index("dom")
    rows, width, head = team * pix, plan.width, plan.head

    for pad in (actp, cotp, act2p):
        fill_pad(plan, pad)
    for slot in range(team):
        actp[slot, width : width + pix, 0:head] = pays[slot][0:pix, 0:head]
        cotp[slot, width : width + pix, 0:head] = pays[slot][0:pix, head : 2 * head]
        tails = pays[slot][0:pix, 2 * head :].astype(F32)
        actp[slot, width : width + pix, head:] = tails[:, 0 : c - head].astype(BF16)
        cotp[slot, width : width + pix, head:] = tails[:, c - head :].astype(BF16)

    for slot in range(d):
        block = logical_of(plan, owner_ref, here ^ slot)
        w1st[block] = unpack_first(plan, slices[slot][0 : plan.first_rows, :].astype(F32))
    flat = jnp.concatenate([w1st[b] for b in range(d)], axis=1)
    zeros = [jnp.zeros((wide - 3 * local, c), F32)] if wide > 3 * local else []
    total = jnp.zeros((rows, wide), F32)
    for ky in range(3):
        taps = [flat[:, (3 * ky + kx) * c : (3 * ky + kx + 1) * c] for kx in range(3)]
        total = total + nt(window(plan, actp, ky), jnp.concatenate(taps + zeros, axis=0).astype(BF16))
    conv = gather_taps(total, plan, 1)
    lane_ok = iota((1, wide), 1) < local
    same = group_matrix(plan, wide, local)
    tails = jnp.concatenate([pays[slot][pix:, 0:c] for slot in range(team)], axis=0)
    row = iota((16, wide), 0)
    bias = jnp.zeros((team, 16, wide), F32)
    for part in range(plan.embed // c):
        product = nt(tails, tw_ref[part]).reshape(team, 16, wide)
        bias = bias + jnp.where(row == part, product, 0.0)
    bias = jnp.sum(bias, axis=1, keepdims=True)
    conv = jnp.where(lane_ok, conv, 0.0).reshape(team, pix, wide) + bias
    off = conv - group_mean(plan, conv.reshape(rows, wide), same)
    inverse = lax.rsqrt(group_mean(plan, (off * off).reshape(rows, wide), same) + NORM_EPS)
    norm = off * inverse
    norm = norm.reshape(rows, wide)
    gate = 1.0 / (1.0 + jnp.exp(-norm))
    act2x = spread_taps(norm * gate, plan, 1)
    act2p[:, width : width + pix, :] = act2x.astype(BF16).reshape(team, pix, wide)

    for slot in range(d):
        block = logical_of(plan, owner_ref, here ^ slot)
        w2st[block] = unpack_second(plan, slices[slot][plan.first_rows :, :].astype(F32))
    flat = jnp.concatenate([w2st[b][0 : plan.piece] for b in range(d)], axis=0)
    for ky in range(3):
        value = flat[3 * local * ky : 3 * local * (ky + 1)]
        if 3 * local < wide:
            value = jnp.concatenate([value, jnp.zeros((wide - 3 * local, c), F32)], axis=0)
        w2_ref[ky * wide : (ky + 1) * wide, :] = value.astype(BF16)

    back = jnp.zeros((rows, wide), F32)
    for ky in range(3):
        back = back + nt(window(plan, cotp, 2 - ky), w2_ref[ky * wide : (ky + 1) * wide, :])
    back = jnp.where(lane_ok, gather_taps(back, plan, -1), 0.0)
    grad = back * gate * (1.0 + norm * (1.0 - gate))
    grad_mean = group_mean(plan, grad, same)
    prod_mean = group_mean(plan, grad * norm, same)
    shaped = (team, pix, wide)
    grad = inverse * (grad.reshape(shaped) - grad_mean - norm.reshape(shaped) * prod_mean)
    grad = jnp.where(lane_ok, grad, 0.0).reshape(rows, wide).astype(BF16).astype(F32)

    gradt = spread_taps(grad, plan, -1).T.astype(BF16)
    parts = [nn(gradt, window(plan, actp, ky)) for ky in range(3)]
    flat = [parts[t // 3][(t % 3) * local : (t % 3 + 1) * local] for t in range(9)]
    flat = jnp.concatenate(flat, axis=1)
    for block in range(d):
        value = flat[:, block * plan.block_rows : (block + 1) * plan.block_rows]
        held[block, 0 : plan.first_rows, :] = pack_first(plan, value)

    act2t = act2x.T.astype(BF16)
    flat = [nn(act2t, window(plan, cotp, 2 - ky))[0 : 3 * local] for ky in range(3)]
    rest = jnp.zeros((plan.piece_pad - plan.piece, c), F32)
    flat = jnp.concatenate([*flat, rest] if rest.shape[0] else flat, axis=0)
    for block in range(d):
        value = flat[block * plan.piece : block * plan.piece + plan.piece_pad]
        held[block, plan.first_rows :, :] = pack_second(plan, value)
    for slot in range(d):
        piece = held[logical_of(plan, owner_ref, here ^ slot)]
        pieces[slot][...] = piece.astype(pieces[slot].dtype)


def share_kernel(plan, act2p, w2_ref, after_ref, keep_ref, away_ref):
    del after_ref
    team, c, pix, wide = plan.team, plan.channels, plan.pixels, plan.wide
    out = jnp.zeros((team * pix, c), F32)
    for ky in range(3):
        out = out + nn(window(plan, act2p, ky), w2_ref[ky * wide : (ky + 1) * wide, :])
    out = out.reshape(team, pix, c)
    for slot in range(team):
        if slot % 2:
            away_ref[slot // 2] = out[slot].astype(BF16)
        else:
            keep_ref[slot // 2] = out[slot]


def pair_kernel(keep_ref, came_ref, *outs):
    for k, out in enumerate(outs):
        out[...] = (keep_ref[k] + came_ref[k].astype(F32)).astype(out.dtype)


def total_kernel(n, *refs):
    total = refs[0][...].astype(F32)
    for ref in refs[1:n]:
        total = total + ref[...].astype(F32)
    refs[-1][...] = total.astype(refs[-1].dtype)


def stack_kernel(*refs):
    for k, ref in enumerate(refs[:-1]):
        refs[-1][k] = ref[...]


def last_kernel(plan, scale, n_stacks, *refs):
    team, local, c, r = plan.team, plan.local, plan.channels, plan.block_rows
    stacks = refs[0:n_stacks]
    table1_ref, table2_ref, x_ref = refs[n_stacks : n_stacks + 3]
    shares = refs[n_stacks + 3 : -8]
    first_any, second_any, output_ref, held1, held2, first_ref, second_ref, sems = refs[-8:]
    spot = own_spot(plan)
    for slot in range(team):
        piece = stacks[slot % n_stacks][slot // n_stacks, plan.first_rows :, :].astype(F32)
        held2[spot ^ slot] = unpack_second(plan, piece).astype(BF16)
    second_ref[...] = tn(held2[...].reshape(team * plan.piece_pad, c), table2_ref[...]) * scale
    copy2 = pltpu.make_async_copy(second_ref, second_any, sems.at[0])
    copy2.start()
    for slot in range(team):
        piece = stacks[slot % n_stacks][slot // n_stacks, 0 : plan.first_rows, :].astype(F32)
        held1[spot ^ slot] = unpack_first(plan, piece)
    stacked = held1[...].reshape(team * local, r).astype(BF16)
    first_ref[...] = nn(table1_ref[...], stacked) * scale
    copy1 = pltpu.make_async_copy(first_ref, first_any, sems.at[1])
    copy1.start()
    total = x_ref[...].astype(F32)
    for ref in shares:
        total = total + ref[...].reshape(total.shape).astype(F32)
    output_ref[...] = total.astype(BF16)
    copy2.wait()
    copy1.wait()


VMEM = pl.BlockSpec(memory_space=pltpu.VMEM)
SMEM = pl.BlockSpec(memory_space=pltpu.SMEM)


HBM = pl.BlockSpec(memory_space=pltpu.HBM)


def call(kernel, name, out_shape, operands, cost, n_smem=0, n_hbm=0, scratch=(), limit=48 * 1024 * 1024, out_hbm=0):
    n = len(operands)
    return pl.pallas_call(
        kernel,
        name=name,
        out_shape=out_shape,
        in_specs=[SMEM] * n_smem + [HBM] * n_hbm + [VMEM] * (n - n_smem - n_hbm),
        out_specs=[HBM] * out_hbm + [VMEM] * (len(out_shape) - out_hbm) if isinstance(out_shape, tuple) else VMEM,
        scratch_shapes=list(scratch),
        compiler_params=pltpu.CompilerParams(vmem_limit_bytes=limit),
        cost_estimate=pl.CostEstimate(
            flops=int(cost * 1e9), bytes_accessed=int(cost * 3e6), transcendentals=0
        ),
    )(*operands)


def shape(dims, dtype):
    return jax.ShapeDtypeStruct(dims, dtype)


def body(block_input, cotangent, timesteps, owner_map, time_weight, first_weight, second_weight):
    n_rep, n_dom = lax.axis_size("rep"), lax.axis_size("dom")
    height, width, c = block_input.shape[1:]
    plan = Plan(n_rep, n_dom, height, width, c, time_weight.shape[0], first_weight.shape[0])
    team, d, pix = plan.team, n_dom, plan.pixels
    r, local = plan.block_rows, plan.local
    def to_rep(value, step):
        return lax.ppermute(value, "rep", [(i, i ^ step) for i in range(n_rep)])

    def to_dom(value, step):
        return lax.ppermute(value, "dom", [(i, i ^ step) for i in range(d)])

    def team_gather(value):
        slots = [value] + [None] * (team - 1)
        for step in range(2, team, 2):
            slots[step] = to_rep(value, step)
        if team > 1:
            for step in range(0, team, 2):
                slots[step + 1] = to_rep(slots[step], 1)
        return slots

    x = block_input.reshape(pix, c)
    cot = cotangent.reshape(pix, c)
    pay = call(
        functools.partial(slice_kernel, plan),
        "slices",
        shape((plan.first_rows + plan.second_rows, plan.packed), BF16),
        (first_weight.T, second_weight.T),
        2,
        n_hbm=2,
        scratch=(
            pltpu.VMEM((c, r), BF16),
            pltpu.VMEM((c, r), BF16),
            pltpu.SemaphoreType.DMA((2,)),
        ),
        limit=56_000_000,
    )
    act = call(
        functools.partial(act_kernel, plan),
        "act",
        shape((plan.act_rows, 2 * c), BF16),
        (timesteps, x, cot, pay),
        2,
        n_smem=1,
        n_hbm=2,
        scratch=(
            pltpu.VMEM((pix, c), BF16),
            pltpu.VMEM((pix, c), BF16),
            pltpu.SemaphoreType.DMA((2,)),
        ),
        limit=56_000_000,
    )
    pays = team_gather(act)
    slots = {0: pay, d // 2: to_dom(pay, d // 2)}
    if d > 2:
        slots[d // 4] = to_dom(pay, d // 4)
    slots[d // 2] = call(
        relay_kernel,
        "relay",
        shape(pay.shape, BF16),
        (slots[d // 2], *([slots[d // 4]] if d > 2 else [])),
        20,
    )
    time_own, table1, table2 = call(
        functools.partial(time_kernel, plan),
        "time_own",
        (
            shape((plan.embed // c, plan.wide, c), BF16),
            shape((c, team * local), BF16),
            shape((team * plan.piece_pad, r), BF16),
        ),
        (time_weight.T,),
        0.001,
    )
    bit = d // 4
    while bit:
        for slot, value in list(slots.items()):
            if slot + bit not in slots:
                slots[slot + bit] = to_dom(value, bit)
        bit //= 2
    slices = [slots[slot] for slot in range(d)]
    rows = (height + 2) * width
    both = (plan.first_rows + plan.second_rows, plan.packed)
    act2p, w2, *pieces = call(
        functools.partial(main_kernel, plan),
        "main",
        (
            shape((team, rows, plan.wide), BF16),
            shape((3 * plan.wide, c), BF16),
            *[shape(both, BF16 if slot else F32) for slot in range(d)],
        ),
        (owner_map, *pays, *slices, time_own),
        6,
        n_smem=1,
        scratch=(
            pltpu.VMEM((team, rows, c), BF16),
            pltpu.VMEM((team, rows, c), BF16),
            pltpu.VMEM((d, local, r), F32),
            pltpu.VMEM((d, plan.piece_pad, c), F32),
            pltpu.VMEM((d, *both), F32),
        ),
    )

    half = -(-team // 2)
    keep, away = call(
        functools.partial(share_kernel, plan),
        "share",
        (shape((half, pix, c), F32), shape((half, pix, c), BF16)),
        (act2p, w2, pieces[0]),
        0.001,
    )
    shares = [keep]
    if team > 1:
        pairs = call(
            pair_kernel,
            "pair",
            tuple(shape((pix, c), BF16 if k else F32) for k in range(half)),
            (keep, to_rep(away, 1)),
            0.001,
        )
        shares = [pairs[0]] + [to_rep(pairs[k], 2 * k) for k in range(1, half)]

    parts = [pieces[0]] + [to_dom(pieces[step], step) for step in range(1, d)]
    total = call(
        functools.partial(total_kernel, d),
        "total",
        shape(both, BF16 if n_rep == team else F32),
        (*parts, *shares[1:]),
        0.001,
    )

    scale = 1.0 / (n_rep * n_dom)
    same_spot = [[i * team + k for i in range(n_rep // team)] for k in range(team)]
    if n_rep > team:
        total = lax.psum(total, "rep", axis_index_groups=same_spot).astype(BF16)
    stacks = [total[None]]
    if team > 1:
        slots = [total] + [to_rep(total, step) for step in range(2, team, 2)]
        stack = call(stack_kernel, "stack", shape((len(slots), *both), BF16), slots, 0.001)
        stacks = [stack, to_rep(stack, 1)]
    first, second, output = call(
        functools.partial(last_kernel, plan, scale, len(stacks)),
        "last",
        (shape((c, r), F32), shape((c, r), F32), shape((pix, c), BF16)),
        (*stacks, table1, table2, x, *shares),
        0.1,
        scratch=(
            pltpu.VMEM((team, local, r), F32),
            pltpu.VMEM((team, plan.piece_pad, c), BF16),
            pltpu.VMEM((c, r), F32),
            pltpu.VMEM((c, r), F32),
            pltpu.SemaphoreType.DMA((2,)),
        ),
        out_hbm=2,
    )
    return output.reshape(1, height, width, c), first.T, second.T


def solution(mesh):
    placed = (
        P(("rep", "dom"), None, None, None),
        P(("rep", "dom"), None, None, None),
        P(("rep", "dom")),
        P(),
        P(),
        P("dom", None),
        P("dom", None),
    )
    return jax.shard_map(
        body,
        mesh=mesh,
        in_specs=placed,
        out_specs=(P(("rep", "dom"), None, None, None), P("dom", None), P("dom", None)),
        check_vma=False,
    )
```

```python
import functools
import math

import jax
import jax.numpy as jnp
from jax import lax
from jax.experimental import pallas as pl
from jax.experimental.pallas import tpu as pltpu
from jax.sharding import PartitionSpec as P

GROUPS = 32
NORM_EPS = 1e-05
F32 = jnp.float32
BF16 = jnp.bfloat16


def round_up(value, unit):
    return -(-value // unit) * unit


def nn(a, b):
    return lax.dot_general(a, b, (((1,), (0,)), ((), ())), preferred_element_type=F32)


def nt(a, b):
    return lax.dot_general(a, b, (((1,), (1,)), ((), ())), preferred_element_type=F32)


def tn(a, b):
    return lax.dot_general(a, b, (((0,), (0,)), ((), ())), preferred_element_type=F32)


def iota(shape, axis):
    return lax.broadcasted_iota(jnp.int32, shape, axis)


def quotient(value, unit):
    return jnp.floor((value.astype(F32) + 0.5) * (1.0 / unit)).astype(jnp.int32)


def one_hot(hit):
    return jnp.where(hit, 1.0, 0.0).astype(BF16)


def silu(value):
    return value / (1.0 + jnp.exp(-value))


class Plan:
    def __init__(self, n_rep, n_dom, height, width, channels, embed, block_rows):
        if n_dom < 2 or n_dom & (n_dom - 1):
            raise ValueError("dom size")
        self.n_rep, self.n_dom = n_rep, n_dom
        self.height, self.width, self.channels = height, width, channels
        self.embed, self.block_rows = embed, block_rows
        self.pixels = height * width
        self.per_group = channels // GROUPS
        team = 1
        while (
            n_rep % (2 * team) == 0
            and GROUPS % (2 * team) == 0
            and block_rows % (2 * team * self.per_group) == 0
        ):
            team *= 2
        self.team = team
        self.local = channels // team
        self.stretch = self.per_group * team
        self.stretches = block_rows // self.stretch
        self.quarters = channels // self.stretch
        self.piece = self.stretches * self.per_group
        self.piece_pad = round_up(self.piece, 16)
        self.wide = round_up(3 * self.local, 128)
        self.act_rows = self.pixels + 16
        self.head = channels // 128 * 128
        self.packed = 2 * channels
        more = block_rows - self.packed
        if more > 0:
            self.first_rows = self.local + folded_rows(self, self.local, more)
        else:
            self.first_rows = folded_rows(self, self.local, block_rows)
        self.first_rows = round_up(self.first_rows, 16)
        self.second_rows = round_up(folded_rows(self, self.piece_pad, channels), 16)


def own_spot(plan):
    return lax.rem(lax.axis_index("rep"), plan.team)


def logical_of(plan, owner_ref, holder):
    total = 0
    for block in range(plan.n_dom):
        total = total + jnp.where(owner_ref[block] == holder, block, 0)
    return total


def group_matrix(plan, lanes, channels):
    row, col = iota((lanes, lanes), 0), iota((lanes, lanes), 1)
    same = quotient(row, plan.per_group) == quotient(col, plan.per_group)
    return one_hot(same & (row < channels) & (col < channels))


def group_sum(sums, same):
    rows = sums.shape[0]
    if rows < 8:
        sums = jnp.concatenate([sums, jnp.zeros((8 - rows, sums.shape[1]), F32)], axis=0)
    high = sums.astype(BF16).astype(F32)
    mid = (sums - high).astype(BF16).astype(F32)
    parts = jnp.concatenate([high, mid, sums - high - mid, jnp.zeros_like(high)], axis=0)
    total = nn(parts.astype(BF16), same)
    return (total[0:8] + total[8:16] + total[16:24])[0:rows]


def fold(plan, value):
    rows, lanes = value.shape
    fits = plan.packed // lanes
    chunk = round_up(-(-rows // fits), 8)
    if chunk * fits > rows:
        value = jnp.concatenate([value, jnp.zeros((chunk * fits - rows, lanes), F32)], axis=0)
    parts = [value[i * chunk : (i + 1) * chunk] for i in range(fits)]
    if fits * lanes < plan.packed:
        parts.append(jnp.zeros((chunk, plan.packed - fits * lanes), F32))
    return parts[0] if len(parts) == 1 else jnp.concatenate(parts, axis=1)


def unfold(plan, value, rows, lanes):
    fits = plan.packed // lanes
    parts = [value[:, i * lanes : (i + 1) * lanes] for i in range(fits)]
    return jnp.concatenate(parts, axis=0)[0:rows]


def folded_rows(plan, rows, lanes):
    return round_up(-(-rows // (plan.packed // lanes)), 8)


def pack_first(plan, value):
    if plan.block_rows > plan.packed:
        parts = [value[:, 0 : plan.packed], fold(plan, value[:, plan.packed :])]
    else:
        parts = [fold(plan, value)]
    have = sum(part.shape[0] for part in parts)
    if have < plan.first_rows:
        parts.append(jnp.zeros((plan.first_rows - have, plan.packed), F32))
    return jnp.concatenate(parts, axis=0) if len(parts) > 1 else parts[0]


def unpack_first(plan, value):
    local, r = plan.local, plan.block_rows
    if r > plan.packed:
        more = r - plan.packed
        tail = unfold(plan, value[local : local + folded_rows(plan, local, more)], local, more)
        return jnp.concatenate([value[0:local], tail], axis=1)
    return unfold(plan, value[0 : folded_rows(plan, local, r)], local, r)


def pack_second(plan, value):
    value = fold(plan, value)
    if value.shape[0] < plan.second_rows:
        rest = jnp.zeros((plan.second_rows - value.shape[0], plan.packed), F32)
        value = jnp.concatenate([value, rest], axis=0)
    return value


def unpack_second(plan, value):
    rows = folded_rows(plan, plan.piece_pad, plan.channels)
    return unfold(plan, value[0:rows], plan.piece_pad, plan.channels)


def local_to_global(plan, index, spot):
    band = quotient(index, plan.per_group)
    return band * plan.stretch + spot * plan.per_group + index - band * plan.per_group


def slice_kernel(plan, w1_any, w2_any, pay_ref, w1_ref, w2_ref, sems):
    copies = [
        pltpu.make_async_copy(src, dst, sems.at[i])
        for i, (src, dst) in enumerate(((w1_any, w1_ref), (w2_any, w2_ref)))
    ]
    for copy in copies:
        copy.start()
    spot = own_spot(plan)
    row, col = iota((plan.local, plan.channels), 0), iota((plan.local, plan.channels), 1)
    pick1 = one_hot(col == local_to_global(plan, row, spot))
    lanes = round_up(plan.piece_pad, 128)
    row, col = iota((plan.block_rows, lanes), 0), iota((plan.block_rows, lanes), 1)
    pick2 = one_hot((row == local_to_global(plan, col, spot)) & (col < plan.piece))
    copies[0].wait()
    pay_ref[0 : plan.first_rows, :] = pack_first(plan, nn(pick1, w1_ref[...])).astype(BF16)
    copies[1].wait()
    pay_ref[plan.first_rows :, :] = pack_second(plan, nn(w2_ref[...], pick2).T[0 : plan.piece_pad]).astype(BF16)


def act_kernel(plan, x_any, cot_any, steps_ref, after_ref, act_ref, x_ref, cot_ref, sems):
    del after_ref
    copies = [
        pltpu.make_async_copy(src, dst, sems.at[i])
        for i, (src, dst) in enumerate(((x_any, x_ref), (cot_any, cot_ref)))
    ]
    for copy in copies:
        copy.start()
    c, pix, head = plan.channels, plan.pixels, plan.head
    same = group_matrix(plan, c, c)
    count = pix * plan.per_group
    copies[0].wait()
    x = x_ref[...].astype(F32)
    off = x - group_sum(jnp.sum(x, 0, keepdims=True), same) / count
    spread = group_sum(jnp.sum(off * off, 0, keepdims=True), same) / count
    act = silu(off * lax.rsqrt(spread + NORM_EPS)).astype(BF16)
    copies[1].wait()
    act_ref[0:pix, 0:head] = act[:, 0:head]
    act_ref[0:pix, head : 2 * head] = cot_ref[:, 0:head]
    act_ref[0:pix, 2 * head :] = jnp.concatenate(
        [act[:, head:].astype(F32), cot_ref[:, head:].astype(F32)], axis=1
    ).astype(BF16)
    half = plan.embed // 2
    k = iota((16, c), 0) * c + iota((16, c), 1)
    angle = jnp.where(k < half, k, k - half).astype(F32)
    angle = steps_ref[...].astype(F32) * jnp.exp(-math.log(10000.0) * angle / half)
    wave = silu(jnp.where(k < half, jnp.cos(angle), jnp.sin(angle)))
    wave = jnp.where(iota((16, c), 0) < plan.embed // c, wave, 0.0)
    act_ref[pix:, :] = jnp.concatenate([wave, jnp.zeros((16, c), F32)], axis=1).astype(BF16)


def relay_kernel(pass_ref, *refs):
    refs[-1][...] = pass_ref[...]


def time_kernel(plan, tw_ref, out_ref, main_ref, fold_ref, second_ref):
    c = plan.channels
    spot = own_spot(plan)
    row, col = iota((plan.wide, c), 0), iota((plan.wide, c), 1)
    pick = one_hot((row < plan.local) & (col == local_to_global(plan, row, spot)))
    own = nn(pick, tw_ref[...])
    for part in range(plan.embed // c):
        out_ref[part] = own[:, part * c : (part + 1) * c].astype(BF16)

    n = -(-plan.team // 2)
    base, chunk, used, _ = fold_layout(plan)
    for kind in range(main_ref.shape[0]):

        def holder(place):
            return (2 * place + kind) ^ spot

        row, col = iota(main_ref.shape[1:], 0), iota(main_ref.shape[1:], 1)
        place = quotient(col, plan.first_rows)
        inner = col - place * plan.first_rows
        hit = (inner < plan.local) & (row == local_to_global(plan, inner, holder(place)))
        main_ref[kind] = one_hot(hit)
        row, col = iota(fold_ref.shape[1:], 0), iota(fold_ref.shape[1:], 1)
        piece = quotient(col, n * chunk)
        place = quotient(col - piece * (n * chunk), chunk)
        inner = col - (piece * n + place - piece) * chunk
        hit = (inner < plan.local) & (row == local_to_global(plan, inner, holder(place)))
        fold_ref[kind] = one_hot(hit)
        row, col = iota(second_ref.shape[1:], 0), iota(second_ref.shape[1:], 1)
        piece = quotient(row, n * plan.second_rows)
        place = quotient(row - piece * (n * plan.second_rows), plan.second_rows)
        inner = row - (piece * n + place) * plan.second_rows
        rows = folded_rows(plan, plan.piece_pad, c)
        hit = (inner < rows) & (inner + piece * rows < plan.piece)
        hit = hit & (col == local_to_global(plan, inner + piece * rows, holder(place)))
        second_ref[kind] = one_hot(hit)


def roll_rows(value, shift, width, plan):
    rows = value.shape[0]
    moved = pltpu.roll(value, shift % rows, 0)
    x = iota(value.shape, 0) & (width - 1) if width & (width - 1) == 0 else lax.rem(iota(value.shape, 0), width)
    return jnp.where(x == (0 if shift == 1 else width - 1), 0.0, moved)


def roll_lanes(value, shift):
    lanes = value.shape[1]
    return value if shift % lanes == 0 else pltpu.roll(value, shift % lanes, 1)


def gather_taps(wide, plan, sign):
    left = roll_rows(wide, sign, plan.width, plan)
    right = roll_rows(roll_lanes(wide, -2 * plan.local), -sign, plan.width, plan)
    return left + roll_lanes(wide, -plan.local) + right


def spread_taps(value, plan, sign):
    left = roll_rows(value, sign, plan.width, plan)
    right = roll_rows(value, -sign, plan.width, plan)
    return left + roll_lanes(value, plan.local) + roll_lanes(right, 2 * plan.local)


def window(plan, pad, tap):
    value = pad[:, tap * plan.width : tap * plan.width + plan.pixels, :]
    return value.reshape(value.shape[0] * plan.pixels, value.shape[2])


def fill_pad(plan, pad):
    pad[:, 0 : plan.width, :] = jnp.zeros((pad.shape[0], plan.width, pad.shape[2]), BF16)
    pad[:, plan.width + plan.pixels :, :] = jnp.zeros((pad.shape[0], plan.width, pad.shape[2]), BF16)


def group_mean(plan, value, same):
    team, wide = plan.team, plan.wide
    sums = jnp.sum(value.reshape(team, plan.pixels, wide), axis=1)
    sums = [group_sum(sums[k : k + 8], same) for k in range(0, team, 8)]
    sums = sums[0] if len(sums) == 1 else jnp.concatenate(sums, axis=0)
    return sums.reshape(team, 1, wide) * (1.0 / (plan.pixels * plan.per_group))


def row_taps(plan, value, sign):
    team, pix, wide, width = plan.team, plan.pixels, plan.wide, plan.width
    value = value.reshape(team, pix, 3 * wide)
    edge = jnp.zeros((team, width, wide), F32)
    low, mid, high = (value[:, :, k * wide : (k + 1) * wide] for k in range(3))
    if sign < 0:
        low, high = high, low
    low = jnp.concatenate([edge, low[:, : pix - width]], axis=1)
    high = jnp.concatenate([high[:, width:], edge], axis=1)
    return (low + mid + high).reshape(team * pix, wide)


def stack_rows(plan, value, sign):
    width, pix = plan.width, plan.pixels
    lanes = value.shape[1]
    inside = lax.rem(iota(value.shape, 1), pix)
    above = jnp.where(inside < width, 0.0, pltpu.roll(value, width, 1))
    below = jnp.where(inside >= pix - width, 0.0, pltpu.roll(value, lanes - width, 1))
    order = (above, value, below) if sign > 0 else (below, value, above)
    return jnp.concatenate([part.astype(BF16) for part in order], axis=0)


def main_kernel(plan, owner_ref, *refs):
    team, d, c, pix, local, wide = plan.team, plan.n_dom, plan.channels, plan.pixels, plan.local, plan.wide
    pays, slices, tw_ref = refs[0:team], refs[team : team + d], refs[team + d]
    act2p, w2_ref = refs[team + d + 1 : team + d + 3]
    pieces = refs[team + d + 3 : team + 2 * d + 3]
    maps, w1st, w2st, held = refs[team + 2 * d + 3 :]
    here = lax.axis_index("dom")
    rows, width, head = team * pix, plan.width, plan.head
    tail = c - head

    for slot in range(team):
        maps[slot * pix : (slot + 1) * pix, :] = pays[slot][0:pix, :]

    for slot in range(d):
        block = logical_of(plan, owner_ref, here ^ slot)
        w1st[block] = unpack_first(plan, slices[slot][0 : plan.first_rows, :].astype(F32))
        w2st[block] = unpack_second(plan, slices[slot][plan.first_rows :, :].astype(F32))
    flat = jnp.concatenate([w1st[b] for b in range(d)], axis=1)
    zeros = [jnp.zeros((wide - 3 * local, c), F32)] if wide > 3 * local else []
    w1 = []
    for ky in range(3):
        w1 += [flat[:, t * c : (t + 1) * c] for t in range(3 * ky, 3 * ky + 3)] + zeros
    w1 = jnp.concatenate(w1, axis=0)
    flat = jnp.concatenate([w2st[b][0 : plan.piece] for b in range(d)], axis=0)
    w2 = []
    for ky in range(3):
        w2 += [flat[3 * local * ky : 3 * local * (ky + 1)]] + zeros
    w2 = jnp.concatenate(w2, axis=0)
    w2_ref[...] = w2.astype(BF16)

    lane_ok = iota((1, wide), 1) < local
    same = group_matrix(plan, wide, local)
    none = jnp.zeros((3 * wide, tail), F32)
    w1_tail = jnp.concatenate([w1[:, head:], none], axis=1).astype(BF16)
    w2_tail = jnp.concatenate([none, w2[:, head:]], axis=1).astype(BF16)
    conv = nt(maps[:, 0:head], w1[:, 0:head].astype(BF16)) + nt(maps[:, 2 * head :], w1_tail)
    conv = gather_taps(row_taps(plan, conv, 1), plan, 1)
    tails = jnp.concatenate([pays[slot][pix:, 0:c] for slot in range(team)], axis=0)
    row = iota((16, wide), 0)
    bias = jnp.zeros((team, 16, wide), F32)
    for part in range(plan.embed // c):
        product = nt(tails, tw_ref[part]).reshape(team, 16, wide)
        bias = bias + jnp.where(row == part, product, 0.0)
    bias = jnp.sum(bias, axis=1, keepdims=True)
    conv = jnp.where(lane_ok, conv, 0.0).reshape(team, pix, wide) + bias
    off = conv - group_mean(plan, conv.reshape(rows, wide), same)
    inverse = lax.rsqrt(group_mean(plan, (off * off).reshape(rows, wide), same) + NORM_EPS)
    norm = (off * inverse).reshape(rows, wide)
    gate = 1.0 / (1.0 + jnp.exp(-norm))
    act2x = spread_taps(norm * gate, plan, 1)
    fill_pad(plan, act2p)
    act2p[:, width : width + pix, :] = act2x.astype(BF16).reshape(team, pix, wide)

    back = nt(maps[:, head : 2 * head], w2[:, 0:head].astype(BF16)) + nt(maps[:, 2 * head :], w2_tail)
    back = jnp.where(lane_ok, gather_taps(row_taps(plan, back, -1), plan, -1), 0.0)
    grad = back * gate * (1.0 + norm * (1.0 - gate))
    grad_mean = group_mean(plan, grad, same)
    prod_mean = group_mean(plan, grad * norm, same)
    shaped = (team, pix, wide)
    grad = inverse * (grad.reshape(shaped) - grad_mean - norm.reshape(shaped) * prod_mean)
    grad = jnp.where(lane_ok, grad, 0.0).reshape(rows, wide).astype(BF16).astype(F32)

    act2t = stack_rows(plan, act2x.T, 1)
    gradt = stack_rows(plan, spread_taps(grad, plan, -1).T, -1)
    tails = nn(jnp.concatenate([gradt, act2t], axis=0), maps[:, 2 * head :])
    first = jnp.concatenate([nn(gradt, maps[:, 0:head]), tails[0 : 3 * wide, 0:tail]], axis=1)
    second = jnp.concatenate([nn(act2t, maps[:, head : 2 * head]), tails[3 * wide :, tail:]], axis=1)
    flat = []
    for t in range(9):
        start = t // 3 * wide + t % 3 * local
        flat.append(first[start : start + local])
    flat = jnp.concatenate(flat, axis=1)
    for block in range(d):
        value = flat[:, block * plan.block_rows : (block + 1) * plan.block_rows]
        held[block, 0 : plan.first_rows, :] = pack_first(plan, value)
    flat = [second[ky * wide : ky * wide + 3 * local] for ky in range(3)]
    rest = jnp.zeros((plan.piece_pad - plan.piece, c), F32)
    flat = jnp.concatenate([*flat, rest] if rest.shape[0] else flat, axis=0)
    for block in range(d):
        value = flat[block * plan.piece : block * plan.piece + plan.piece_pad]
        held[block, plan.first_rows :, :] = pack_second(plan, value)
    for slot in range(d):
        piece = held[logical_of(plan, owner_ref, here ^ slot)]
        pieces[slot][...] = piece.astype(pieces[slot].dtype)


def share_kernel(plan, act2p, w2_ref, after_ref, keep_ref, away_ref):
    del after_ref
    team, c, pix, wide = plan.team, plan.channels, plan.pixels, plan.wide
    out = jnp.zeros((team * pix, c), F32)
    for ky in range(3):
        out = out + nn(window(plan, act2p, ky), w2_ref[ky * wide : (ky + 1) * wide, :])
    out = out.reshape(team, pix, c)
    for slot in range(team):
        if slot % 2:
            away_ref[slot // 2] = out[slot].astype(BF16)
        else:
            keep_ref[slot // 2] = out[slot]


def pair_kernel(keep_ref, came_ref, *outs):
    for k, out in enumerate(outs):
        out[...] = (keep_ref[k] + came_ref[k].astype(F32)).astype(out.dtype)


def total_kernel(n, *refs):
    total = refs[0][...].astype(F32)
    for ref in refs[1:n]:
        total = total + ref[...].astype(F32)
    refs[-1][...] = total.astype(refs[-1].dtype)


def stack_kernel(*refs):
    for k, ref in enumerate(refs[:-1]):
        refs[-1][k] = ref[...]


def fold_layout(plan):
    more = plan.block_rows - plan.packed
    base, lanes = (plan.local, more) if more > 0 else (0, plan.block_rows)
    chunk = folded_rows(plan, plan.local, lanes)
    return base, chunk, -(-plan.local // chunk), lanes


def first_in_place(plan, stack_ref, main_table, fold_table):
    n = stack_ref.shape[0]
    base, chunk, used, lanes = fold_layout(plan)
    folded = stack_ref[:, base : base + chunk, :].astype(F32).reshape(n * chunk, plan.packed)
    folded = [folded[:, k * lanes : (k + 1) * lanes] for k in range(used)]
    first = nn(fold_table, jnp.concatenate(folded, axis=0).astype(BF16))
    if not base:
        return first
    rows = stack_ref[:, 0 : plan.first_rows, :].reshape(n * plan.first_rows, plan.packed)
    return jnp.concatenate([nn(main_table, rows), first], axis=1)


def second_in_place(plan, stack_ref, table):
    n, c = stack_ref.shape[0], plan.channels
    rows = stack_ref[:, plan.first_rows :, :].reshape(n * plan.second_rows, plan.packed)
    rows = [rows[:, k * c : (k + 1) * c] for k in range(plan.packed // c)]
    return tn(jnp.concatenate(rows, axis=0), table)


def part_kernel(plan, stack_ref, main_ref, fold_ref, second_ref, out1_ref, out2_ref):
    out1_ref[...] = first_in_place(plan, stack_ref, main_ref[0], fold_ref[0])
    out2_ref[...] = second_in_place(plan, stack_ref, second_ref[0])


def last_kernel(plan, scale, n_came, *refs):
    came, tables, part1_ref, part2_ref, x_ref = refs[0:n_came], refs[n_came : n_came + 3], *refs[n_came + 3 : n_came + 6]
    shares = refs[n_came + 6 : -7]
    first_any, second_any, output_any, first_ref, second_ref, output_ref, sems = refs[-7:]
    total = x_ref[...].astype(F32)
    for ref in shares:
        total = total + ref[...].reshape(total.shape).astype(F32)
    output_ref[...] = total.astype(BF16)
    copy0 = pltpu.make_async_copy(output_ref, output_any, sems.at[2])
    copy0.start()
    first = part1_ref[...]
    for ref in came:
        first = first + first_in_place(plan, ref, tables[0][1], tables[1][1])
    first_ref[...] = first * scale
    copy1 = pltpu.make_async_copy(first_ref, first_any, sems.at[0])
    copy1.start()
    second = part2_ref[...]
    for ref in came:
        second = second + second_in_place(plan, ref, tables[2][1])
    second_ref[...] = second * scale
    copy2 = pltpu.make_async_copy(second_ref, second_any, sems.at[1])
    copy2.start()
    copy0.wait()
    copy1.wait()
    copy2.wait()


VMEM = pl.BlockSpec(memory_space=pltpu.VMEM)
SMEM = pl.BlockSpec(memory_space=pltpu.SMEM)


HBM = pl.BlockSpec(memory_space=pltpu.HBM)


def call(kernel, name, out_shape, operands, cost, n_smem=0, n_hbm=0, scratch=(), limit=48 * 1024 * 1024, out_hbm=0):
    n = len(operands)
    return pl.pallas_call(
        kernel,
        name=name,
        out_shape=out_shape,
        in_specs=[SMEM] * n_smem + [HBM] * n_hbm + [VMEM] * (n - n_smem - n_hbm),
        out_specs=[HBM] * out_hbm + [VMEM] * (len(out_shape) - out_hbm) if isinstance(out_shape, tuple) else VMEM,
        scratch_shapes=list(scratch),
        compiler_params=pltpu.CompilerParams(vmem_limit_bytes=limit),
        cost_estimate=pl.CostEstimate(
            flops=int(cost * 1e9), bytes_accessed=int(cost * 3e6), transcendentals=0
        ),
    )(*operands)


def shape(dims, dtype):
    return jax.ShapeDtypeStruct(dims, dtype)


def body(block_input, cotangent, timesteps, owner_map, time_weight, first_weight, second_weight):
    n_rep, n_dom = lax.axis_size("rep"), lax.axis_size("dom")
    height, width, c = block_input.shape[1:]
    plan = Plan(n_rep, n_dom, height, width, c, time_weight.shape[0], first_weight.shape[0])
    team, d, pix = plan.team, n_dom, plan.pixels
    r, local = plan.block_rows, plan.local
    def to_rep(value, step):
        return lax.ppermute(value, "rep", [(i, i ^ step) for i in range(n_rep)])

    def to_dom(value, step):
        return lax.ppermute(value, "dom", [(i, i ^ step) for i in range(d)])

    def team_gather(value):
        slots = [value] + [None] * (team - 1)
        for step in range(2, team, 2):
            slots[step] = to_rep(value, step)
        if team > 1:
            for step in range(0, team, 2):
                slots[step + 1] = to_rep(slots[step], 1)
        return slots

    x = block_input.reshape(pix, c)
    cot = cotangent.reshape(pix, c)
    pay = call(
        functools.partial(slice_kernel, plan),
        "slices",
        shape((plan.first_rows + plan.second_rows, plan.packed), BF16),
        (first_weight.T, second_weight.T),
        2,
        n_hbm=2,
        scratch=(
            pltpu.VMEM((c, r), BF16),
            pltpu.VMEM((c, r), BF16),
            pltpu.SemaphoreType.DMA((2,)),
        ),
        limit=56_000_000,
    )
    act = call(
        functools.partial(act_kernel, plan),
        "act",
        shape((plan.act_rows, 2 * c), BF16),
        (x, cot, timesteps.reshape(1, 1), pay),
        2,
        n_hbm=2,
        scratch=(
            pltpu.VMEM((pix, c), BF16),
            pltpu.VMEM((pix, c), BF16),
            pltpu.SemaphoreType.DMA((2,)),
        ),
        limit=56_000_000,
    )
    pays = team_gather(act)
    slots = {0: pay, d // 2: to_dom(pay, d // 2)}
    if d > 2:
        slots[d // 4] = to_dom(pay, d // 4)
    slots[d // 2] = call(
        relay_kernel,
        "relay",
        shape(pay.shape, BF16),
        (slots[d // 2], *([slots[d // 4]] if d > 2 else [])),
        20,
    )
    kinds, half = min(team, 2), -(-team // 2)
    _, chunk, used, _ = fold_layout(plan)
    time_own, *tables = call(
        functools.partial(time_kernel, plan),
        "time_own",
        (
            shape((plan.embed // c, plan.wide, c), BF16),
            shape((kinds, c, half * plan.first_rows), BF16),
            shape((kinds, c, half * chunk * used), BF16),
            shape((kinds, plan.packed // c * half * plan.second_rows, r), BF16),
        ),
        (time_weight.T,),
        0.001,
    )
    bit = d // 4
    while bit:
        for slot, value in list(slots.items()):
            if slot + bit not in slots:
                slots[slot + bit] = to_dom(value, bit)
        bit //= 2
    slices = [slots[slot] for slot in range(d)]
    rows = (height + 2) * width
    both = (plan.first_rows + plan.second_rows, plan.packed)
    act2p, w2, *pieces = call(
        functools.partial(main_kernel, plan),
        "main",
        (
            shape((team, rows, plan.wide), BF16),
            shape((3 * plan.wide, c), BF16),
            *[shape(both, BF16 if slot else F32) for slot in range(d)],
        ),
        (owner_map, *pays, *slices, time_own),
        6,
        n_smem=1,
        scratch=(
            pltpu.VMEM((team * pix, 2 * c), BF16),
            pltpu.VMEM((d, local, r), F32),
            pltpu.VMEM((d, plan.piece_pad, c), F32),
            pltpu.VMEM((d, *both), F32),
        ),
    )

    keep, away = call(
        functools.partial(share_kernel, plan),
        "share",
        (shape((half, pix, c), F32), shape((half, pix, c), BF16)),
        (act2p, w2, pieces[0]),
        0.001,
    )
    shares = [keep]
    if team > 1:
        pairs = call(
            pair_kernel,
            "pair",
            tuple(shape((pix, c), BF16 if k else F32) for k in range(half)),
            (keep, to_rep(away, 1)),
            0.001,
        )
        shares = [pairs[0]] + [to_rep(pairs[k], 2 * k) for k in range(1, half)]

    parts = [pieces[0]] + [to_dom(pieces[step], step) for step in range(1, d)]
    total = call(
        functools.partial(total_kernel, d),
        "total",
        shape(both, BF16 if n_rep == team else F32),
        (*parts, *shares[1:]),
        0.001,
    )

    scale = 1.0 / (n_rep * n_dom)
    same_spot = [[i * team + k for i in range(n_rep // team)] for k in range(team)]
    if n_rep > team:
        total = lax.psum(total, "rep", axis_index_groups=same_spot).astype(BF16)
    stack, came = total[None], []
    if team > 1:
        slots = [total] + [to_rep(total, step) for step in range(2, team, 2)]
        stack = call(stack_kernel, "stack", shape((half, *both), BF16), slots, 0.001)
        came = [to_rep(stack, 1)]
    part1, part2 = call(
        functools.partial(part_kernel, plan),
        "part",
        (shape((c, r), F32), shape((c, r), F32)),
        (stack, *tables),
        0.001,
    )
    first, second, output = call(
        functools.partial(last_kernel, plan, scale, len(came)),
        "last",
        (shape((c, r), F32), shape((c, r), F32), shape((pix, c), BF16)),
        (*came, *tables, part1, part2, x, *shares),
        0.1,
        scratch=(
            pltpu.VMEM((c, r), F32),
            pltpu.VMEM((c, r), F32),
            pltpu.VMEM((pix, c), BF16),
            pltpu.SemaphoreType.DMA((3,)),
        ),
        out_hbm=3,
    )
    return output.reshape(1, height, width, c), first.T, second.T


def solution(mesh):
    placed = (
        P(("rep", "dom"), None, None, None),
        P(("rep", "dom"), None, None, None),
        P(("rep", "dom")),
        P(),
        P(),
        P("dom", None),
        P("dom", None),
    )
    return jax.shard_map(
        body,
        mesh=mesh,
        in_specs=placed,
        out_specs=(P(("rep", "dom"), None, None, None), P("dom", None), P("dom", None)),
        check_vma=False,
    )
```

```python
import functools
import math

import jax
import jax.numpy as jnp
from jax import lax
from jax.experimental import pallas as pl
from jax.experimental.pallas import tpu as pltpu
from jax.sharding import PartitionSpec as P

GROUPS = 32
NORM_EPS = 1e-05
F32 = jnp.float32
BF16 = jnp.bfloat16


def round_up(value, unit):
    return -(-value // unit) * unit


def nn(a, b):
    return lax.dot_general(a, b, (((1,), (0,)), ((), ())), preferred_element_type=F32)


def nt(a, b):
    return lax.dot_general(a, b, (((1,), (1,)), ((), ())), preferred_element_type=F32)


def tn(a, b):
    return lax.dot_general(a, b, (((0,), (0,)), ((), ())), preferred_element_type=F32)


def iota(shape, axis):
    return lax.broadcasted_iota(jnp.int32, shape, axis)


def quotient(value, unit):
    return jnp.floor((value.astype(F32) + 0.5) * (1.0 / unit)).astype(jnp.int32)


def one_hot(hit):
    return jnp.where(hit, 1.0, 0.0).astype(BF16)


def silu(value):
    return value / (1.0 + jnp.exp(-value))


class Plan:
    def __init__(self, n_rep, n_dom, height, width, channels, embed, block_rows):
        if n_dom < 2 or n_dom & (n_dom - 1):
            raise ValueError("dom size")
        self.n_rep, self.n_dom = n_rep, n_dom
        self.height, self.width, self.channels = height, width, channels
        self.embed, self.block_rows = embed, block_rows
        self.pixels = height * width
        self.per_group = channels // GROUPS
        team = 1
        while (
            n_rep % (2 * team) == 0
            and GROUPS % (2 * team) == 0
            and block_rows % (2 * team * self.per_group) == 0
        ):
            team *= 2
        self.team = team
        self.local = channels // team
        self.stretch = self.per_group * team
        self.stretches = block_rows // self.stretch
        self.quarters = channels // self.stretch
        self.piece = self.stretches * self.per_group
        self.piece_pad = round_up(self.piece, 16)
        self.wide = round_up(3 * self.local, 128)
        self.act_rows = self.pixels + 16
        self.head = channels // 128 * 128
        self.packed = 2 * channels
        more = block_rows - self.packed
        if more > 0:
            self.first_rows = self.local + folded_rows(self, self.local, more)
        else:
            self.first_rows = folded_rows(self, self.local, block_rows)
        self.first_rows = round_up(self.first_rows, 16)
        self.second_rows = round_up(folded_rows(self, self.piece_pad, channels), 16)


def own_spot(plan):
    return lax.rem(lax.axis_index("rep"), plan.team)


def logical_of(plan, owner_ref, holder):
    total = 0
    for block in range(plan.n_dom):
        total = total + jnp.where(owner_ref[block] == holder, block, 0)
    return total


def group_matrix(plan, lanes, channels):
    row, col = iota((lanes, lanes), 0), iota((lanes, lanes), 1)
    same = quotient(row, plan.per_group) == quotient(col, plan.per_group)
    return one_hot(same & (row < channels) & (col < channels))


def group_sum(sums, same):
    rows = sums.shape[0]
    if rows < 8:
        sums = jnp.concatenate([sums, jnp.zeros((8 - rows, sums.shape[1]), F32)], axis=0)
    high = sums.astype(BF16).astype(F32)
    mid = (sums - high).astype(BF16).astype(F32)
    parts = jnp.concatenate([high, mid, sums - high - mid, jnp.zeros_like(high)], axis=0)
    total = nn(parts.astype(BF16), same)
    return (total[0:8] + total[8:16] + total[16:24])[0:rows]


def fold(plan, value):
    rows, lanes = value.shape
    fits = plan.packed // lanes
    chunk = round_up(-(-rows // fits), 8)
    if chunk * fits > rows:
        value = jnp.concatenate([value, jnp.zeros((chunk * fits - rows, lanes), F32)], axis=0)
    parts = [value[i * chunk : (i + 1) * chunk] for i in range(fits)]
    if fits * lanes < plan.packed:
        parts.append(jnp.zeros((chunk, plan.packed - fits * lanes), F32))
    return parts[0] if len(parts) == 1 else jnp.concatenate(parts, axis=1)


def unfold(plan, value, rows, lanes):
    fits = plan.packed // lanes
    parts = [value[:, i * lanes : (i + 1) * lanes] for i in range(fits)]
    return jnp.concatenate(parts, axis=0)[0:rows]


def folded_rows(plan, rows, lanes):
    return round_up(-(-rows // (plan.packed // lanes)), 8)


def pack_first(plan, value):
    if plan.block_rows > plan.packed:
        parts = [value[:, 0 : plan.packed], fold(plan, value[:, plan.packed :])]
    else:
        parts = [fold(plan, value)]
    have = sum(part.shape[0] for part in parts)
    if have < plan.first_rows:
        parts.append(jnp.zeros((plan.first_rows - have, plan.packed), F32))
    return jnp.concatenate(parts, axis=0) if len(parts) > 1 else parts[0]


def unpack_first(plan, value):
    local, r = plan.local, plan.block_rows
    if r > plan.packed:
        more = r - plan.packed
        tail = unfold(plan, value[local : local + folded_rows(plan, local, more)], local, more)
        return jnp.concatenate([value[0:local], tail], axis=1)
    return unfold(plan, value[0 : folded_rows(plan, local, r)], local, r)


def pack_second(plan, value):
    value = fold(plan, value)
    if value.shape[0] < plan.second_rows:
        rest = jnp.zeros((plan.second_rows - value.shape[0], plan.packed), F32)
        value = jnp.concatenate([value, rest], axis=0)
    return value


def unpack_second(plan, value):
    rows = folded_rows(plan, plan.piece_pad, plan.channels)
    return unfold(plan, value[0:rows], plan.piece_pad, plan.channels)


def local_to_global(plan, index, spot):
    band = quotient(index, plan.per_group)
    return band * plan.stretch + spot * plan.per_group + index - band * plan.per_group


def slice_kernel(plan, w1_any, w2_any, pay_ref, w1_ref, w2_ref, sems):
    copies = [
        pltpu.make_async_copy(src, dst, sems.at[i])
        for i, (src, dst) in enumerate(((w1_any, w1_ref), (w2_any, w2_ref)))
    ]
    for copy in copies:
        copy.start()
    spot = own_spot(plan)
    row, col = iota((plan.local, plan.channels), 0), iota((plan.local, plan.channels), 1)
    pick1 = one_hot(col == local_to_global(plan, row, spot))
    lanes = round_up(plan.piece_pad, 128)
    row, col = iota((plan.block_rows, lanes), 0), iota((plan.block_rows, lanes), 1)
    pick2 = one_hot((row == local_to_global(plan, col, spot)) & (col < plan.piece))
    copies[0].wait()
    pay_ref[0 : plan.first_rows, :] = pack_first(plan, nn(pick1, w1_ref[...])).astype(BF16)
    copies[1].wait()
    pay_ref[plan.first_rows : plan.first_rows + plan.second_rows, :] = pack_second(plan, nn(w2_ref[...], pick2).T[0 : plan.piece_pad]).astype(BF16)


def act_kernel(plan, x_any, cot_any, steps_ref, after_ref, act_ref, x_ref, cot_ref, sems):
    del after_ref
    copies = [
        pltpu.make_async_copy(src, dst, sems.at[i])
        for i, (src, dst) in enumerate(((x_any, x_ref), (cot_any, cot_ref)))
    ]
    for copy in copies:
        copy.start()
    c, pix, head = plan.channels, plan.pixels, plan.head
    same = group_matrix(plan, c, c)
    count = pix * plan.per_group
    copies[0].wait()
    x = x_ref[...].astype(F32)
    off = x - group_sum(jnp.sum(x, 0, keepdims=True), same) / count
    spread = group_sum(jnp.sum(off * off, 0, keepdims=True), same) / count
    act = silu(off * lax.rsqrt(spread + NORM_EPS)).astype(BF16)
    copies[1].wait()
    act_ref[0:pix, 0:head] = act[:, 0:head]
    act_ref[0:pix, head : 2 * head] = cot_ref[:, 0:head]
    act_ref[0:pix, 2 * head :] = jnp.concatenate(
        [act[:, head:].astype(F32), cot_ref[:, head:].astype(F32)], axis=1
    ).astype(BF16)
    half = plan.embed // 2
    k = iota((16, c), 0) * c + iota((16, c), 1)
    angle = jnp.where(k < half, k, k - half).astype(F32)
    angle = steps_ref[...].astype(F32) * jnp.exp(-math.log(10000.0) * angle / half)
    wave = silu(jnp.where(k < half, jnp.cos(angle), jnp.sin(angle)))
    wave = jnp.where(iota((16, c), 0) < plan.embed // c, wave, 0.0)
    act_ref[pix:, :] = jnp.concatenate([wave, jnp.zeros((16, c), F32)], axis=1).astype(BF16)


def relay_kernel(pass_ref, *refs):
    refs[-1][...] = pass_ref[0 : refs[-1].shape[0], :]


def time_kernel(plan, tw_ref, out_ref):
    c = plan.channels
    spot = own_spot(plan)
    row, col = iota((plan.wide, c), 0), iota((plan.wide, c), 1)
    pick = one_hot((row < plan.local) & (col == local_to_global(plan, row, spot)))
    own = nn(pick, tw_ref[...])
    for part in range(plan.embed // c):
        out_ref[part] = own[:, part * c : (part + 1) * c].astype(BF16)


def table_kernel(plan, after_ref, main_ref, fold_ref, second_ref):
    del after_ref
    c, spot = plan.channels, own_spot(plan)
    n = -(-plan.team // 2)
    base, chunk, used, _ = fold_layout(plan)
    for kind in range(main_ref.shape[0]):

        def holder(place):
            return (2 * place + kind) ^ spot

        row, col = iota(main_ref.shape[1:], 0), iota(main_ref.shape[1:], 1)
        place = quotient(col, plan.first_rows)
        inner = col - place * plan.first_rows
        hit = (inner < plan.local) & (row == local_to_global(plan, inner, holder(place)))
        main_ref[kind] = one_hot(hit)
        row, col = iota(fold_ref.shape[1:], 0), iota(fold_ref.shape[1:], 1)
        piece = quotient(col, n * chunk)
        place = quotient(col - piece * (n * chunk), chunk)
        inner = col - (piece * n + place - piece) * chunk
        hit = (inner < plan.local) & (row == local_to_global(plan, inner, holder(place)))
        fold_ref[kind] = one_hot(hit)
        row, col = iota(second_ref.shape[1:], 0), iota(second_ref.shape[1:], 1)
        piece = quotient(row, n * plan.second_rows)
        place = quotient(row - piece * (n * plan.second_rows), plan.second_rows)
        inner = row - (piece * n + place) * plan.second_rows
        rows = folded_rows(plan, plan.piece_pad, c)
        hit = (inner < rows) & (inner + piece * rows < plan.piece)
        hit = hit & (col == local_to_global(plan, inner + piece * rows, holder(place)))
        second_ref[kind] = one_hot(hit)


def roll_rows(value, shift, width, plan):
    rows = value.shape[0]
    moved = pltpu.roll(value, shift % rows, 0)
    x = iota(value.shape, 0) & (width - 1) if width & (width - 1) == 0 else lax.rem(iota(value.shape, 0), width)
    return jnp.where(x == (0 if shift == 1 else width - 1), 0.0, moved)


def roll_lanes(value, shift):
    lanes = value.shape[1]
    return value if shift % lanes == 0 else pltpu.roll(value, shift % lanes, 1)


def gather_taps(wide, plan, sign):
    left = roll_rows(wide, sign, plan.width, plan)
    right = roll_rows(roll_lanes(wide, -2 * plan.local), -sign, plan.width, plan)
    return left + roll_lanes(wide, -plan.local) + right


def spread_taps(value, plan, sign):
    left = roll_rows(value, sign, plan.width, plan)
    right = roll_rows(value, -sign, plan.width, plan)
    return left + roll_lanes(value, plan.local) + roll_lanes(right, 2 * plan.local)


def window(plan, pad, tap):
    value = pad[:, tap * plan.width : tap * plan.width + plan.pixels, :]
    return value.reshape(value.shape[0] * plan.pixels, value.shape[2])


def fill_pad(plan, pad):
    pad[:, 0 : plan.width, :] = jnp.zeros((pad.shape[0], plan.width, pad.shape[2]), BF16)
    pad[:, plan.width + plan.pixels :, :] = jnp.zeros((pad.shape[0], plan.width, pad.shape[2]), BF16)


def group_mean(plan, value, same):
    team, wide = plan.team, plan.wide
    sums = jnp.sum(value.reshape(team, plan.pixels, wide), axis=1)
    sums = [group_sum(sums[k : k + 8], same) for k in range(0, team, 8)]
    sums = sums[0] if len(sums) == 1 else jnp.concatenate(sums, axis=0)
    return sums.reshape(team, 1, wide) * (1.0 / (plan.pixels * plan.per_group))


def row_taps(plan, value, sign):
    team, pix, wide, width = plan.team, plan.pixels, plan.wide, plan.width
    value = value.reshape(team, pix, 3 * wide)
    edge = jnp.zeros((team, width, wide), F32)
    low, mid, high = (value[:, :, k * wide : (k + 1) * wide] for k in range(3))
    if sign < 0:
        low, high = high, low
    low = jnp.concatenate([edge, low[:, : pix - width]], axis=1)
    high = jnp.concatenate([high[:, width:], edge], axis=1)
    return (low + mid + high).reshape(team * pix, wide)


def stack_rows(plan, value, sign):
    width, pix = plan.width, plan.pixels
    lanes = value.shape[1]
    inside = lax.rem(iota(value.shape, 1), pix)
    above = jnp.where(inside < width, 0.0, pltpu.roll(value, width, 1))
    below = jnp.where(inside >= pix - width, 0.0, pltpu.roll(value, lanes - width, 1))
    order = (above, value, below) if sign > 0 else (below, value, above)
    return jnp.concatenate([part.astype(BF16) for part in order], axis=0)


def main_kernel(plan, owner_ref, *refs):
    team, d, c, pix, local, wide = plan.team, plan.n_dom, plan.channels, plan.pixels, plan.local, plan.wide
    pays, slices, tw_ref = refs[0:team], refs[team : team + d], refs[team + d]
    act2p, w2_ref = refs[team + d + 1 : team + d + 3]
    pieces = refs[team + d + 3 : team + 2 * d + 3]
    maps, w1st, w2st, held = refs[team + 2 * d + 3 :]
    here = lax.axis_index("dom")
    rows, width, head = team * pix, plan.width, plan.head
    tail = c - head

    for slot in range(team):
        maps[slot * pix : (slot + 1) * pix, :] = pays[slot][0:pix, :]

    for slot in range(d):
        block = logical_of(plan, owner_ref, here ^ slot)
        w1st[block] = unpack_first(plan, slices[slot][0 : plan.first_rows, :].astype(F32))
        w2st[block] = unpack_second(plan, slices[slot][plan.first_rows : plan.first_rows + plan.second_rows, :].astype(F32))
    flat = jnp.concatenate([w1st[b] for b in range(d)], axis=1)
    zeros = [jnp.zeros((wide - 3 * local, c), F32)] if wide > 3 * local else []
    w1 = []
    for ky in range(3):
        w1 += [flat[:, t * c : (t + 1) * c] for t in range(3 * ky, 3 * ky + 3)] + zeros
    w1 = jnp.concatenate(w1, axis=0)
    flat = jnp.concatenate([w2st[b][0 : plan.piece] for b in range(d)], axis=0)
    w2 = []
    for ky in range(3):
        w2 += [flat[3 * local * ky : 3 * local * (ky + 1)]] + zeros
    w2 = jnp.concatenate(w2, axis=0)
    w2_ref[...] = w2.astype(BF16)

    lane_ok = iota((1, wide), 1) < local
    same = group_matrix(plan, wide, local)
    none = jnp.zeros((3 * wide, tail), F32)
    w1_tail = jnp.concatenate([w1[:, head:], none], axis=1).astype(BF16)
    w2_tail = jnp.concatenate([none, w2[:, head:]], axis=1).astype(BF16)
    conv = nt(maps[:, 0:head], w1[:, 0:head].astype(BF16)) + nt(maps[:, 2 * head :], w1_tail)
    conv = gather_taps(row_taps(plan, conv, 1), plan, 1)
    tails = jnp.concatenate([pays[slot][pix:, 0:c] for slot in range(team)], axis=0)
    row = iota((16, wide), 0)
    bias = jnp.zeros((team, 16, wide), F32)
    for part in range(plan.embed // c):
        product = nt(tails, tw_ref[part]).reshape(team, 16, wide)
        bias = bias + jnp.where(row == part, product, 0.0)
    bias = jnp.sum(bias, axis=1, keepdims=True)
    conv = jnp.where(lane_ok, conv, 0.0).reshape(team, pix, wide) + bias
    off = conv - group_mean(plan, conv.reshape(rows, wide), same)
    inverse = lax.rsqrt(group_mean(plan, (off * off).reshape(rows, wide), same) + NORM_EPS)
    norm = (off * inverse).reshape(rows, wide)
    gate = 1.0 / (1.0 + jnp.exp(-norm))
    act2x = spread_taps(norm * gate, plan, 1)
    fill_pad(plan, act2p)
    act2p[:, width : width + pix, :] = act2x.astype(BF16).reshape(team, pix, wide)

    back = nt(maps[:, head : 2 * head], w2[:, 0:head].astype(BF16)) + nt(maps[:, 2 * head :], w2_tail)
    back = jnp.where(lane_ok, gather_taps(row_taps(plan, back, -1), plan, -1), 0.0)
    grad = back * gate * (1.0 + norm * (1.0 - gate))
    grad_mean = group_mean(plan, grad, same)
    prod_mean = group_mean(plan, grad * norm, same)
    shaped = (team, pix, wide)
    grad = inverse * (grad.reshape(shaped) - grad_mean - norm.reshape(shaped) * prod_mean)
    grad = jnp.where(lane_ok, grad, 0.0).reshape(rows, wide).astype(BF16).astype(F32)

    act2t = stack_rows(plan, act2x.T, 1)
    gradt = stack_rows(plan, spread_taps(grad, plan, -1).T, -1)
    tails = nn(jnp.concatenate([gradt, act2t], axis=0), maps[:, 2 * head :])
    first = jnp.concatenate([nn(gradt, maps[:, 0:head]), tails[0 : 3 * wide, 0:tail]], axis=1)
    second = jnp.concatenate([nn(act2t, maps[:, head : 2 * head]), tails[3 * wide :, tail:]], axis=1)
    flat = []
    for t in range(9):
        start = t // 3 * wide + t % 3 * local
        flat.append(first[start : start + local])
    flat = jnp.concatenate(flat, axis=1)
    for block in range(d):
        value = flat[:, block * plan.block_rows : (block + 1) * plan.block_rows]
        held[block, 0 : plan.first_rows, :] = pack_first(plan, value)
    flat = [second[ky * wide : ky * wide + 3 * local] for ky in range(3)]
    rest = jnp.zeros((plan.piece_pad - plan.piece, c), F32)
    flat = jnp.concatenate([*flat, rest] if rest.shape[0] else flat, axis=0)
    for block in range(d):
        value = flat[block * plan.piece : block * plan.piece + plan.piece_pad]
        held[block, plan.first_rows :, :] = pack_second(plan, value)
    for slot in range(d):
        piece = held[logical_of(plan, owner_ref, here ^ slot)]
        pieces[slot][...] = piece.astype(pieces[slot].dtype)


def share_kernel(plan, act2p, w2_ref, after_ref, keep_ref, away_ref):
    del after_ref
    team, c, pix, wide = plan.team, plan.channels, plan.pixels, plan.wide
    out = jnp.zeros((team * pix, c), F32)
    for ky in range(3):
        out = out + nn(window(plan, act2p, ky), w2_ref[ky * wide : (ky + 1) * wide, :])
    out = out.reshape(team, pix, c)
    for slot in range(team):
        if slot % 2:
            away_ref[slot // 2] = out[slot].astype(BF16)
        else:
            keep_ref[slot // 2] = out[slot]


def pair_kernel(keep_ref, came_ref, *outs):
    for k, out in enumerate(outs):
        out[...] = (keep_ref[k] + came_ref[k].astype(F32)).astype(out.dtype)


def total_kernel(n, *refs):
    total = refs[0][...].astype(F32)
    for ref in refs[1:n]:
        total = total + ref[...].astype(F32)
    refs[-1][...] = total.astype(refs[-1].dtype)


def stack_kernel(*refs):
    for k, ref in enumerate(refs[:-1]):
        refs[-1][k] = ref[...]


def fold_layout(plan):
    more = plan.block_rows - plan.packed
    base, lanes = (plan.local, more) if more > 0 else (0, plan.block_rows)
    chunk = folded_rows(plan, plan.local, lanes)
    return base, chunk, -(-plan.local // chunk), lanes


def first_in_place(plan, stack_ref, main_table, fold_table):
    n = stack_ref.shape[0]
    base, chunk, used, lanes = fold_layout(plan)
    folded = stack_ref[:, base : base + chunk, :].astype(F32).reshape(n * chunk, plan.packed)
    folded = [folded[:, k * lanes : (k + 1) * lanes] for k in range(used)]
    first = nn(fold_table, jnp.concatenate(folded, axis=0).astype(BF16))
    if not base:
        return first
    rows = stack_ref[:, 0 : plan.first_rows, :].reshape(n * plan.first_rows, plan.packed)
    return jnp.concatenate([nn(main_table, rows), first], axis=1)


def second_in_place(plan, stack_ref, table):
    n, c = stack_ref.shape[0], plan.channels
    rows = stack_ref[:, plan.first_rows :, :].reshape(n * plan.second_rows, plan.packed)
    rows = [rows[:, k * c : (k + 1) * c] for k in range(plan.packed // c)]
    return tn(jnp.concatenate(rows, axis=0), table)


def part_kernel(plan, stack_ref, main_ref, fold_ref, second_ref, out1_ref, out2_ref):
    out1_ref[...] = first_in_place(plan, stack_ref, main_ref[0], fold_ref[0])
    out2_ref[...] = second_in_place(plan, stack_ref, second_ref[0])


def last_kernel(plan, scale, n_came, *refs):
    came, tables, part1_ref, part2_ref, x_ref = refs[0:n_came], refs[n_came : n_came + 3], *refs[n_came + 3 : n_came + 6]
    shares = refs[n_came + 6 : -7]
    first_any, second_any, output_any, first_ref, second_ref, output_ref, sems = refs[-7:]
    total = x_ref[...].astype(F32)
    for ref in shares:
        total = total + ref[...].reshape(total.shape).astype(F32)
    output_ref[...] = total.astype(BF16)
    copy0 = pltpu.make_async_copy(output_ref, output_any, sems.at[2])
    copy0.start()
    first = part1_ref[...]
    for ref in came:
        first = first + first_in_place(plan, ref, tables[0][1], tables[1][1])
    first_ref[...] = first * scale
    copy1 = pltpu.make_async_copy(first_ref, first_any, sems.at[0])
    copy1.start()
    second = part2_ref[...]
    for ref in came:
        second = second + second_in_place(plan, ref, tables[2][1])
    second_ref[...] = second * scale
    copy2 = pltpu.make_async_copy(second_ref, second_any, sems.at[1])
    copy2.start()
    copy0.wait()
    copy1.wait()
    copy2.wait()


VMEM = pl.BlockSpec(memory_space=pltpu.VMEM)
SMEM = pl.BlockSpec(memory_space=pltpu.SMEM)


HBM = pl.BlockSpec(memory_space=pltpu.HBM)


def call(kernel, name, out_shape, operands, cost, n_smem=0, n_hbm=0, scratch=(), limit=48 * 1024 * 1024, out_hbm=0):
    n = len(operands)
    return pl.pallas_call(
        kernel,
        name=name,
        out_shape=out_shape,
        in_specs=[SMEM] * n_smem + [HBM] * n_hbm + [VMEM] * (n - n_smem - n_hbm),
        out_specs=[HBM] * out_hbm + [VMEM] * (len(out_shape) - out_hbm) if isinstance(out_shape, tuple) else VMEM,
        scratch_shapes=list(scratch),
        compiler_params=pltpu.CompilerParams(vmem_limit_bytes=limit),
        cost_estimate=pl.CostEstimate(
            flops=int(cost * 1e9), bytes_accessed=int(cost * 3e6), transcendentals=0
        ),
    )(*operands)


def shape(dims, dtype):
    return jax.ShapeDtypeStruct(dims, dtype)


def body(block_input, cotangent, timesteps, owner_map, time_weight, first_weight, second_weight):
    n_rep, n_dom = lax.axis_size("rep"), lax.axis_size("dom")
    height, width, c = block_input.shape[1:]
    plan = Plan(n_rep, n_dom, height, width, c, time_weight.shape[0], first_weight.shape[0])
    team, d, pix = plan.team, n_dom, plan.pixels
    r, local = plan.block_rows, plan.local
    def to_rep(value, step):
        return lax.ppermute(value, "rep", [(i, i ^ step) for i in range(n_rep)])

    def to_dom(value, step):
        return lax.ppermute(value, "dom", [(i, i ^ step) for i in range(d)])

    def team_gather(value):
        slots = [value] + [None] * (team - 1)
        for step in range(2, team, 2):
            slots[step] = to_rep(value, step)
        if team > 1:
            for step in range(0, team, 2):
                slots[step + 1] = to_rep(slots[step], 1)
        return slots

    x = block_input.reshape(pix, c)
    cot = cotangent.reshape(pix, c)
    pay = call(
        functools.partial(slice_kernel, plan),
        "slices",
        shape((plan.first_rows + plan.second_rows + 0, plan.packed), BF16),
        (first_weight.T, second_weight.T),
        2,
        n_hbm=2,
        scratch=(
            pltpu.VMEM((c, r), BF16),
            pltpu.VMEM((c, r), BF16),
            pltpu.SemaphoreType.DMA((2,)),
        ),
        limit=56_000_000,
    )
    act = call(
        functools.partial(act_kernel, plan),
        "act",
        shape((plan.act_rows, 2 * c), BF16),
        (x, cot, timesteps.reshape(1, 1), pay),
        2,
        n_hbm=2,
        scratch=(
            pltpu.VMEM((pix, c), BF16),
            pltpu.VMEM((pix, c), BF16),
            pltpu.SemaphoreType.DMA((2,)),
        ),
        limit=56_000_000,
    )
    pays = team_gather(act)
    slots = {0: pay, d // 2: to_dom(pay, d // 2)}
    if d > 2:
        slots[d // 4] = to_dom(pay, d // 4)
    slots[d // 2] = call(
        relay_kernel,
        "relay",
        shape((plan.first_rows + plan.second_rows, plan.packed), BF16),
        (slots[d // 2], *([slots[d // 4]] if d > 2 else [])),
        20,
    )
    kinds, half = min(team, 2), -(-team // 2)
    _, chunk, used, _ = fold_layout(plan)
    time_own = call(
        functools.partial(time_kernel, plan),
        "time_own",
        shape((plan.embed // c, plan.wide, c), BF16),
        (time_weight.T,),
        5,
    )
    bit = d // 4
    while bit:
        for slot, value in list(slots.items()):
            if slot + bit not in slots:
                slots[slot + bit] = to_dom(value, bit)
        bit //= 2
    slices = [slots[slot] for slot in range(d)]
    rows = (height + 2) * width
    both = (plan.first_rows + plan.second_rows, plan.packed)
    act2p, w2, *pieces = call(
        functools.partial(main_kernel, plan),
        "main",
        (
            shape((team, rows, plan.wide), BF16),
            shape((3 * plan.wide, c), BF16),
            *[shape(both, BF16 if slot else F32) for slot in range(d)],
        ),
        (owner_map, *pays, *slices, time_own),
        6,
        n_smem=1,
        scratch=(
            pltpu.VMEM((team * pix, 2 * c), BF16),
            pltpu.VMEM((d, local, r), F32),
            pltpu.VMEM((d, plan.piece_pad, c), F32),
            pltpu.VMEM((d, *both), F32),
        ),
    )

    keep, away = call(
        functools.partial(share_kernel, plan),
        "share",
        (shape((half, pix, c), F32), shape((half, pix, c), BF16)),
        (act2p, w2, pieces[0]),
        0.001,
    )
    shares = [keep]
    if team > 1:
        pairs = call(
            pair_kernel,
            "pair",
            tuple(shape((pix, c), BF16 if k else F32) for k in range(half)),
            (keep, to_rep(away, 1)),
            0.001,
        )
        shares = [pairs[0]] + [to_rep(pairs[k], 2 * k) for k in range(1, half)]

    tables = call(
        functools.partial(table_kernel, plan),
        "tables",
        (
            shape((kinds, c, half * plan.first_rows), BF16),
            shape((kinds, c, half * chunk * used), BF16),
            shape((kinds, plan.packed // c * half * plan.second_rows, r), BF16),
        ),
        (shares[0],),
        0.001,
    )

    parts = [pieces[0]] + [to_dom(pieces[step], step) for step in range(1, d)]
    total = call(
        functools.partial(total_kernel, d),
        "total",
        shape(both, BF16 if n_rep == team else F32),
        (*parts, *shares[1:], tables[0]),
        0.001,
    )

    scale = 1.0 / (n_rep * n_dom)
    same_spot = [[i * team + k for i in range(n_rep // team)] for k in range(team)]
    if n_rep > team:
        total = lax.psum(total, "rep", axis_index_groups=same_spot).astype(BF16)
    stack, came = total[None], []
    if team > 1:
        slots = [total] + [to_rep(total, step) for step in range(2, team, 2)]
        stack = call(stack_kernel, "stack", shape((half, *both), BF16), slots, 0.001)
        came = [to_rep(stack, 1)]
    part1, part2 = call(
        functools.partial(part_kernel, plan),
        "part",
        (shape((c, r), F32), shape((c, r), F32)),
        (stack, *tables),
        0.001,
    )
    first, second, output = call(
        functools.partial(last_kernel, plan, scale, len(came)),
        "last",
        (shape((c, r), F32), shape((c, r), F32), shape((pix, c), BF16)),
        (*came, *tables, part1, part2, x, *shares),
        0.1,
        scratch=(
            pltpu.VMEM((c, r), F32),
            pltpu.VMEM((c, r), F32),
            pltpu.VMEM((pix, c), BF16),
            pltpu.SemaphoreType.DMA((3,)),
        ),
        out_hbm=3,
    )
    return output.reshape(1, height, width, c), first.T, second.T


def solution(mesh):
    placed = (
        P(("rep", "dom"), None, None, None),
        P(("rep", "dom"), None, None, None),
        P(("rep", "dom")),
        P(),
        P(),
        P("dom", None),
        P("dom", None),
    )
    return jax.shard_map(
        body,
        mesh=mesh,
        in_specs=placed,
        out_specs=(P(("rep", "dom"), None, None, None), P("dom", None), P("dom", None)),
        check_vma=False,
    )
```

```python
import functools
import math

import jax
import jax.numpy as jnp
from jax import lax
from jax.experimental import pallas as pl
from jax.experimental.pallas import tpu as pltpu
from jax.sharding import PartitionSpec as P

GROUPS = 32
NORM_EPS = 1e-05
F32 = jnp.float32
BF16 = jnp.bfloat16


def round_up(value, unit):
    return -(-value // unit) * unit


def nn(a, b):
    return lax.dot_general(a, b, (((1,), (0,)), ((), ())), preferred_element_type=F32)


def nt(a, b):
    return lax.dot_general(a, b, (((1,), (1,)), ((), ())), preferred_element_type=F32)


def tn(a, b):
    return lax.dot_general(a, b, (((0,), (0,)), ((), ())), preferred_element_type=F32)


def iota(shape, axis):
    return lax.broadcasted_iota(jnp.int32, shape, axis)


def quotient(value, unit):
    return jnp.floor((value.astype(F32) + 0.5) * (1.0 / unit)).astype(jnp.int32)


def one_hot(hit):
    return jnp.where(hit, 1.0, 0.0).astype(BF16)


def silu(value):
    return value / (1.0 + jnp.exp(-value))


class Plan:
    def __init__(self, n_rep, n_dom, height, width, channels, embed, block_rows):
        if n_dom < 2 or n_dom & (n_dom - 1):
            raise ValueError("dom size")
        self.n_rep, self.n_dom = n_rep, n_dom
        self.height, self.width, self.channels = height, width, channels
        self.embed, self.block_rows = embed, block_rows
        self.pixels = height * width
        self.per_group = channels // GROUPS
        team = 1
        while (
            n_rep % (2 * team) == 0
            and GROUPS % (2 * team) == 0
            and block_rows % (2 * team * self.per_group) == 0
        ):
            team *= 2
        self.team = team
        self.local = channels // team
        self.stretch = self.per_group * team
        self.stretches = block_rows // self.stretch
        self.quarters = channels // self.stretch
        self.piece = self.stretches * self.per_group
        self.piece_pad = round_up(self.piece, 16)
        self.wide = round_up(3 * self.local, 128)
        self.act_rows = self.pixels + 16
        self.head = channels // 128 * 128
        self.packed = 2 * channels
        more = block_rows - self.packed
        if more > 0:
            self.first_rows = self.local + folded_rows(self, self.local, more)
        else:
            self.first_rows = folded_rows(self, self.local, block_rows)
        self.first_rows = round_up(self.first_rows, 16)
        self.second_rows = round_up(folded_rows(self, self.piece_pad, channels), 16)


def own_spot(plan):
    return lax.rem(lax.axis_index("rep"), plan.team)


def logical_of(plan, owner_ref, holder):
    total = 0
    for block in range(plan.n_dom):
        total = total + jnp.where(owner_ref[block] == holder, block, 0)
    return total


def group_matrix(plan, lanes, channels):
    row, col = iota((lanes, lanes), 0), iota((lanes, lanes), 1)
    same = quotient(row, plan.per_group) == quotient(col, plan.per_group)
    return one_hot(same & (row < channels) & (col < channels))


def group_sum(sums, same):
    rows = sums.shape[0]
    if rows < 8:
        sums = jnp.concatenate([sums, jnp.zeros((8 - rows, sums.shape[1]), F32)], axis=0)
    high = sums.astype(BF16).astype(F32)
    mid = (sums - high).astype(BF16).astype(F32)
    parts = jnp.concatenate([high, mid, sums - high - mid, jnp.zeros_like(high)], axis=0)
    total = nn(parts.astype(BF16), same)
    return (total[0:8] + total[8:16] + total[16:24])[0:rows]


def fold(plan, value):
    rows, lanes = value.shape
    fits = plan.packed // lanes
    chunk = round_up(-(-rows // fits), 8)
    if chunk * fits > rows:
        value = jnp.concatenate([value, jnp.zeros((chunk * fits - rows, lanes), F32)], axis=0)
    parts = [value[i * chunk : (i + 1) * chunk] for i in range(fits)]
    if fits * lanes < plan.packed:
        parts.append(jnp.zeros((chunk, plan.packed - fits * lanes), F32))
    return parts[0] if len(parts) == 1 else jnp.concatenate(parts, axis=1)


def unfold(plan, value, rows, lanes):
    fits = plan.packed // lanes
    parts = [value[:, i * lanes : (i + 1) * lanes] for i in range(fits)]
    return jnp.concatenate(parts, axis=0)[0:rows]


def folded_rows(plan, rows, lanes):
    return round_up(-(-rows // (plan.packed // lanes)), 8)


def pack_first(plan, value):
    if plan.block_rows > plan.packed:
        parts = [value[:, 0 : plan.packed], fold(plan, value[:, plan.packed :])]
    else:
        parts = [fold(plan, value)]
    have = sum(part.shape[0] for part in parts)
    if have < plan.first_rows:
        parts.append(jnp.zeros((plan.first_rows - have, plan.packed), F32))
    return jnp.concatenate(parts, axis=0) if len(parts) > 1 else parts[0]


def unpack_first(plan, value):
    local, r = plan.local, plan.block_rows
    if r > plan.packed:
        more = r - plan.packed
        tail = unfold(plan, value[local : local + folded_rows(plan, local, more)], local, more)
        return jnp.concatenate([value[0:local], tail], axis=1)
    return unfold(plan, value[0 : folded_rows(plan, local, r)], local, r)


def pack_second(plan, value):
    value = fold(plan, value)
    if value.shape[0] < plan.second_rows:
        rest = jnp.zeros((plan.second_rows - value.shape[0], plan.packed), F32)
        value = jnp.concatenate([value, rest], axis=0)
    return value


def unpack_second(plan, value):
    rows = folded_rows(plan, plan.piece_pad, plan.channels)
    return unfold(plan, value[0:rows], plan.piece_pad, plan.channels)


def local_to_global(plan, index, spot):
    band = quotient(index, plan.per_group)
    return band * plan.stretch + spot * plan.per_group + index - band * plan.per_group


def slice_kernel(plan, w1_any, w2_any, pay_ref, w1_ref, w2_ref, sems):
    copies = [
        pltpu.make_async_copy(src, dst, sems.at[i])
        for i, (src, dst) in enumerate(((w1_any, w1_ref), (w2_any, w2_ref)))
    ]
    for copy in copies:
        copy.start()
    spot = own_spot(plan)
    row, col = iota((plan.local, plan.channels), 0), iota((plan.local, plan.channels), 1)
    pick1 = one_hot(col == local_to_global(plan, row, spot))
    lanes = round_up(plan.piece_pad, 128)
    row, col = iota((plan.block_rows, lanes), 0), iota((plan.block_rows, lanes), 1)
    pick2 = one_hot((row == local_to_global(plan, col, spot)) & (col < plan.piece))
    copies[0].wait()
    pay_ref[0 : plan.first_rows, :] = pack_first(plan, nn(pick1, w1_ref[...])).astype(BF16)
    copies[1].wait()
    pay_ref[plan.first_rows : plan.first_rows + plan.second_rows, :] = pack_second(plan, nn(w2_ref[...], pick2).T[0 : plan.piece_pad]).astype(BF16)


def act_kernel(plan, x_ref, cot_ref, steps_ref, after_ref, act_ref):
    del after_ref
    c, pix, head = plan.channels, plan.pixels, plan.head
    same = group_matrix(plan, c, c)
    count = pix * plan.per_group
    x = x_ref[...].astype(F32)
    off = x - group_sum(jnp.sum(x, 0, keepdims=True), same) / count
    spread = group_sum(jnp.sum(off * off, 0, keepdims=True), same) / count
    act = silu(off * lax.rsqrt(spread + NORM_EPS)).astype(BF16)
    act_ref[0:pix, 0:head] = act[:, 0:head]
    act_ref[0:pix, head : 2 * head] = cot_ref[:, 0:head]
    act_ref[0:pix, 2 * head :] = jnp.concatenate(
        [act[:, head:].astype(F32), cot_ref[:, head:].astype(F32)], axis=1
    ).astype(BF16)
    half = plan.embed // 2
    k = iota((16, c), 0) * c + iota((16, c), 1)
    angle = jnp.where(k < half, k, k - half).astype(F32)
    angle = steps_ref[...].astype(F32) * jnp.exp(-math.log(10000.0) * angle / half)
    wave = silu(jnp.where(k < half, jnp.cos(angle), jnp.sin(angle)))
    wave = jnp.where(iota((16, c), 0) < plan.embed // c, wave, 0.0)
    act_ref[pix:, :] = jnp.concatenate([wave, jnp.zeros((16, c), F32)], axis=1).astype(BF16)


def relay_kernel(pass_ref, *refs):
    refs[-1][...] = pass_ref[0 : refs[-1].shape[0], :]


def time_kernel(plan, tw_ref, out_ref):
    c = plan.channels
    spot = own_spot(plan)
    row, col = iota((plan.wide, c), 0), iota((plan.wide, c), 1)
    pick = one_hot((row < plan.local) & (col == local_to_global(plan, row, spot)))
    own = nn(pick, tw_ref[...])
    for part in range(plan.embed // c):
        out_ref[part] = own[:, part * c : (part + 1) * c].astype(BF16)


def table_kernel(plan, after_ref, main_ref, fold_ref, second_ref):
    del after_ref
    c, spot = plan.channels, own_spot(plan)
    n = -(-plan.team // 2)
    base, chunk, used, _ = fold_layout(plan)
    for kind in range(main_ref.shape[0]):

        def holder(place):
            return (2 * place + kind) ^ spot

        row, col = iota(main_ref.shape[1:], 0), iota(main_ref.shape[1:], 1)
        place = quotient(col, plan.first_rows)
        inner = col - place * plan.first_rows
        hit = (inner < plan.local) & (row == local_to_global(plan, inner, holder(place)))
        main_ref[kind] = one_hot(hit)
        row, col = iota(fold_ref.shape[1:], 0), iota(fold_ref.shape[1:], 1)
        piece = quotient(col, n * chunk)
        place = quotient(col - piece * (n * chunk), chunk)
        inner = col - (piece * n + place - piece) * chunk
        hit = (inner < plan.local) & (row == local_to_global(plan, inner, holder(place)))
        fold_ref[kind] = one_hot(hit)
        row, col = iota(second_ref.shape[1:], 0), iota(second_ref.shape[1:], 1)
        piece = quotient(row, n * plan.second_rows)
        place = quotient(row - piece * (n * plan.second_rows), plan.second_rows)
        inner = row - (piece * n + place) * plan.second_rows
        rows = folded_rows(plan, plan.piece_pad, c)
        hit = (inner < rows) & (inner + piece * rows < plan.piece)
        hit = hit & (col == local_to_global(plan, inner + piece * rows, holder(place)))
        second_ref[kind] = one_hot(hit)


def roll_rows(value, shift, width, plan):
    rows = value.shape[0]
    moved = pltpu.roll(value, shift % rows, 0)
    x = iota(value.shape, 0) & (width - 1) if width & (width - 1) == 0 else lax.rem(iota(value.shape, 0), width)
    return jnp.where(x == (0 if shift == 1 else width - 1), 0.0, moved)


def roll_lanes(value, shift):
    lanes = value.shape[1]
    return value if shift % lanes == 0 else pltpu.roll(value, shift % lanes, 1)


def gather_taps(wide, plan, sign):
    left = roll_rows(wide, sign, plan.width, plan)
    right = roll_rows(roll_lanes(wide, -2 * plan.local), -sign, plan.width, plan)
    return left + roll_lanes(wide, -plan.local) + right


def spread_taps(value, plan, sign):
    left = roll_rows(value, sign, plan.width, plan)
    right = roll_rows(value, -sign, plan.width, plan)
    return left + roll_lanes(value, plan.local) + roll_lanes(right, 2 * plan.local)


def window(plan, pad, tap):
    value = pad[:, tap * plan.width : tap * plan.width + plan.pixels, :]
    return value.reshape(value.shape[0] * plan.pixels, value.shape[2])


def fill_pad(plan, pad):
    pad[:, 0 : plan.width, :] = jnp.zeros((pad.shape[0], plan.width, pad.shape[2]), BF16)
    pad[:, plan.width + plan.pixels :, :] = jnp.zeros((pad.shape[0], plan.width, pad.shape[2]), BF16)


def group_mean(plan, value, same):
    team, wide = plan.team, plan.wide
    sums = jnp.sum(value.reshape(team, plan.pixels, wide), axis=1)
    sums = [group_sum(sums[k : k + 8], same) for k in range(0, team, 8)]
    sums = sums[0] if len(sums) == 1 else jnp.concatenate(sums, axis=0)
    return sums.reshape(team, 1, wide) * (1.0 / (plan.pixels * plan.per_group))


def row_taps(plan, value, sign):
    team, pix, wide, width = plan.team, plan.pixels, plan.wide, plan.width
    value = value.reshape(team, pix, 3 * wide)
    edge = jnp.zeros((team, width, wide), F32)
    low, mid, high = (value[:, :, k * wide : (k + 1) * wide] for k in range(3))
    if sign < 0:
        low, high = high, low
    low = jnp.concatenate([edge, low[:, : pix - width]], axis=1)
    high = jnp.concatenate([high[:, width:], edge], axis=1)
    return (low + mid + high).reshape(team * pix, wide)


def stack_rows(plan, value, sign):
    width, pix = plan.width, plan.pixels
    lanes = value.shape[1]
    inside = lax.rem(iota(value.shape, 1), pix)
    above = jnp.where(inside < width, 0.0, pltpu.roll(value, width, 1))
    below = jnp.where(inside >= pix - width, 0.0, pltpu.roll(value, lanes - width, 1))
    order = (above, value, below) if sign > 0 else (below, value, above)
    return jnp.concatenate([part.astype(BF16) for part in order], axis=0)


def main_kernel(plan, owner_ref, *refs):
    team, d, c, pix, local, wide = plan.team, plan.n_dom, plan.channels, plan.pixels, plan.local, plan.wide
    pays, slices, tw_ref = refs[0:team], refs[team : team + d], refs[team + d]
    act2p, w2_ref = refs[team + d + 1 : team + d + 3]
    pieces = refs[team + d + 3 : team + 2 * d + 3]
    maps, w1st, w2st, held = refs[team + 2 * d + 3 :]
    here = lax.axis_index("dom")
    rows, width, head = team * pix, plan.width, plan.head
    tail = c - head

    for slot in range(team):
        maps[slot * pix : (slot + 1) * pix, :] = pays[slot][0:pix, :]

    for slot in range(d):
        block = logical_of(plan, owner_ref, here ^ slot)
        w1st[block] = unpack_first(plan, slices[slot][0 : plan.first_rows, :].astype(F32))
        w2st[block] = unpack_second(plan, slices[slot][plan.first_rows : plan.first_rows + plan.second_rows, :].astype(F32))
    flat = jnp.concatenate([w1st[b] for b in range(d)], axis=1)
    zeros = [jnp.zeros((wide - 3 * local, c), F32)] if wide > 3 * local else []
    w1 = []
    for ky in range(3):
        w1 += [flat[:, t * c : (t + 1) * c] for t in range(3 * ky, 3 * ky + 3)] + zeros
    w1 = jnp.concatenate(w1, axis=0)
    flat = jnp.concatenate([w2st[b][0 : plan.piece] for b in range(d)], axis=0)
    w2 = []
    for ky in range(3):
        w2 += [flat[3 * local * ky : 3 * local * (ky + 1)]] + zeros
    w2 = jnp.concatenate(w2, axis=0)
    w2_ref[...] = w2.astype(BF16)

    lane_ok = iota((1, wide), 1) < local
    same = group_matrix(plan, wide, local)
    none = jnp.zeros((3 * wide, tail), F32)
    w1_tail = jnp.concatenate([w1[:, head:], none], axis=1).astype(BF16)
    w2_tail = jnp.concatenate([none, w2[:, head:]], axis=1).astype(BF16)
    conv = nt(maps[:, 0:head], w1[:, 0:head].astype(BF16)) + nt(maps[:, 2 * head :], w1_tail)
    conv = gather_taps(row_taps(plan, conv, 1), plan, 1)
    tails = jnp.concatenate([pays[slot][pix:, 0:c] for slot in range(team)], axis=0)
    row = iota((16, wide), 0)
    bias = jnp.zeros((team, 16, wide), F32)
    for part in range(plan.embed // c):
        product = nt(tails, tw_ref[part]).reshape(team, 16, wide)
        bias = bias + jnp.where(row == part, product, 0.0)
    bias = jnp.sum(bias, axis=1, keepdims=True)
    conv = jnp.where(lane_ok, conv, 0.0).reshape(team, pix, wide) + bias
    off = conv - group_mean(plan, conv.reshape(rows, wide), same)
    inverse = lax.rsqrt(group_mean(plan, (off * off).reshape(rows, wide), same) + NORM_EPS)
    norm = (off * inverse).reshape(rows, wide)
    gate = 1.0 / (1.0 + jnp.exp(-norm))
    act2x = spread_taps(norm * gate, plan, 1)
    fill_pad(plan, act2p)
    act2p[:, width : width + pix, :] = act2x.astype(BF16).reshape(team, pix, wide)

    back = nt(maps[:, head : 2 * head], w2[:, 0:head].astype(BF16)) + nt(maps[:, 2 * head :], w2_tail)
    back = jnp.where(lane_ok, gather_taps(row_taps(plan, back, -1), plan, -1), 0.0)
    grad = back * gate * (1.0 + norm * (1.0 - gate))
    grad_mean = group_mean(plan, grad, same)
    prod_mean = group_mean(plan, grad * norm, same)
    shaped = (team, pix, wide)
    grad = inverse * (grad.reshape(shaped) - grad_mean - norm.reshape(shaped) * prod_mean)
    grad = jnp.where(lane_ok, grad, 0.0).reshape(rows, wide).astype(BF16).astype(F32)

    act2t = stack_rows(plan, act2x.T, 1)
    gradt = stack_rows(plan, spread_taps(grad, plan, -1).T, -1)
    tails = nn(jnp.concatenate([gradt, act2t], axis=0), maps[:, 2 * head :])
    first = jnp.concatenate([nn(gradt, maps[:, 0:head]), tails[0 : 3 * wide, 0:tail]], axis=1)
    second = jnp.concatenate([nn(act2t, maps[:, head : 2 * head]), tails[3 * wide :, tail:]], axis=1)
    flat = []
    for t in range(9):
        start = t // 3 * wide + t % 3 * local
        flat.append(first[start : start + local])
    flat = jnp.concatenate(flat, axis=1)
    for block in range(d):
        value = flat[:, block * plan.block_rows : (block + 1) * plan.block_rows]
        held[block, 0 : plan.first_rows, :] = pack_first(plan, value)
    flat = [second[ky * wide : ky * wide + 3 * local] for ky in range(3)]
    rest = jnp.zeros((plan.piece_pad - plan.piece, c), F32)
    flat = jnp.concatenate([*flat, rest] if rest.shape[0] else flat, axis=0)
    for block in range(d):
        value = flat[block * plan.piece : block * plan.piece + plan.piece_pad]
        held[block, plan.first_rows :, :] = pack_second(plan, value)
    for slot in range(d):
        piece = held[logical_of(plan, owner_ref, here ^ slot)]
        pieces[slot][...] = piece.astype(pieces[slot].dtype)


def share_kernel(plan, act2p, w2_ref, after_ref, keep_ref, away_ref):
    del after_ref
    team, c, pix = plan.team, plan.channels, plan.pixels
    out = nn(jnp.concatenate([window(plan, act2p, ky) for ky in range(3)], axis=1), w2_ref[...])
    out = out.reshape(team, pix, c)
    for slot in range(team):
        if slot % 2:
            away_ref[slot // 2] = out[slot].astype(BF16)
        else:
            keep_ref[slot // 2] = out[slot]


def pair_kernel(keep_ref, came_ref, *outs):
    for k, out in enumerate(outs):
        out[...] = (keep_ref[k] + came_ref[k].astype(F32)).astype(out.dtype)


def total_kernel(n, *refs):
    total = refs[0][...].astype(F32)
    for ref in refs[1:n]:
        total = total + ref[...].astype(F32)
    refs[-1][...] = total.astype(refs[-1].dtype)


def stack_kernel(*refs):
    for k, ref in enumerate(refs[:-1]):
        refs[-1][k] = ref[...]


def fold_layout(plan):
    more = plan.block_rows - plan.packed
    base, lanes = (plan.local, more) if more > 0 else (0, plan.block_rows)
    chunk = folded_rows(plan, plan.local, lanes)
    return base, chunk, -(-plan.local // chunk), lanes


def first_in_place(plan, stack_ref, main_table, fold_table):
    n = stack_ref.shape[0]
    base, chunk, used, lanes = fold_layout(plan)
    low = base // 16 * 16
    folded = stack_ref[:, low : round_up(base + chunk, 16), :].astype(F32)
    folded = folded[:, base - low : base - low + chunk].reshape(n * chunk, plan.packed)
    folded = [folded[:, k * lanes : (k + 1) * lanes] for k in range(used)]
    first = nn(fold_table, jnp.concatenate(folded, axis=0).astype(BF16))
    if not base:
        return first
    rows = stack_ref[:, 0 : plan.first_rows, :].reshape(n * plan.first_rows, plan.packed)
    return jnp.concatenate([nn(main_table, rows), first], axis=1)


def second_in_place(plan, stack_ref, table):
    n, c = stack_ref.shape[0], plan.channels
    rows = stack_ref[:, plan.first_rows :, :].reshape(n * plan.second_rows, plan.packed)
    rows = [rows[:, k * c : (k + 1) * c] for k in range(plan.packed // c)]
    return tn(jnp.concatenate(rows, axis=0), table)


def part_kernel(plan, stack_ref, main_ref, fold_ref, second_ref, out1_ref, out2_ref):
    out1_ref[...] = first_in_place(plan, stack_ref, main_ref[0], fold_ref[0])
    out2_ref[...] = second_in_place(plan, stack_ref, second_ref[0])


def last_kernel(plan, scale, n_came, *refs):
    came, tables, part1_ref, part2_ref, x_ref = refs[0:n_came], refs[n_came : n_came + 3], *refs[n_came + 3 : n_came + 6]
    shares = refs[n_came + 6 : -7]
    first_any, second_any, output_any, first_ref, second_ref, output_ref, sems = refs[-7:]
    total = x_ref[...].astype(F32)
    for ref in shares:
        total = total + ref[...].reshape(total.shape).astype(F32)
    output_ref[...] = total.astype(BF16)
    copy0 = pltpu.make_async_copy(output_ref, output_any, sems.at[2])
    copy0.start()
    first = part1_ref[...]
    for ref in came:
        first = first + first_in_place(plan, ref, tables[0][1], tables[1][1])
    first_ref[...] = first * scale
    copy1 = pltpu.make_async_copy(first_ref, first_any, sems.at[0])
    copy1.start()
    second = part2_ref[...]
    for ref in came:
        second = second + second_in_place(plan, ref, tables[2][1])
    second_ref[...] = second * scale
    copy2 = pltpu.make_async_copy(second_ref, second_any, sems.at[1])
    copy2.start()
    copy0.wait()
    copy1.wait()
    copy2.wait()


VMEM = pl.BlockSpec(memory_space=pltpu.VMEM)
SMEM = pl.BlockSpec(memory_space=pltpu.SMEM)


HBM = pl.BlockSpec(memory_space=pltpu.HBM)


def call(kernel, name, out_shape, operands, cost, n_smem=0, n_hbm=0, scratch=(), limit=48 * 1024 * 1024, out_hbm=0):
    n = len(operands)
    return pl.pallas_call(
        kernel,
        name=name,
        out_shape=out_shape,
        in_specs=[SMEM] * n_smem + [HBM] * n_hbm + [VMEM] * (n - n_smem - n_hbm),
        out_specs=[HBM] * out_hbm + [VMEM] * (len(out_shape) - out_hbm) if isinstance(out_shape, tuple) else VMEM,
        scratch_shapes=list(scratch),
        compiler_params=pltpu.CompilerParams(vmem_limit_bytes=limit),
        cost_estimate=pl.CostEstimate(
            flops=int(cost * 1e9), bytes_accessed=int(cost * 3e6), transcendentals=0
        ),
    )(*operands)


def shape(dims, dtype):
    return jax.ShapeDtypeStruct(dims, dtype)


def body(block_input, cotangent, timesteps, owner_map, time_weight, first_weight, second_weight):
    n_rep, n_dom = lax.axis_size("rep"), lax.axis_size("dom")
    height, width, c = block_input.shape[1:]
    plan = Plan(n_rep, n_dom, height, width, c, time_weight.shape[0], first_weight.shape[0])
    team, d, pix = plan.team, n_dom, plan.pixels
    r, local = plan.block_rows, plan.local
    def to_rep(value, step):
        return lax.ppermute(value, "rep", [(i, i ^ step) for i in range(n_rep)])

    def to_dom(value, step):
        return lax.ppermute(value, "dom", [(i, i ^ step) for i in range(d)])

    def team_gather(value):
        slots = [value] + [None] * (team - 1)
        for step in range(2, team, 2):
            slots[step] = to_rep(value, step)
        if team > 1:
            for step in range(0, team, 2):
                slots[step + 1] = to_rep(slots[step], 1)
        return slots

    x = block_input.reshape(pix, c)
    cot = cotangent.reshape(pix, c)
    pay = call(
        functools.partial(slice_kernel, plan),
        "slices",
        shape((plan.first_rows + plan.second_rows + 0, plan.packed), BF16),
        (first_weight.T, second_weight.T),
        2,
        n_hbm=2,
        scratch=(
            pltpu.VMEM((c, r), BF16),
            pltpu.VMEM((c, r), BF16),
            pltpu.SemaphoreType.DMA((2,)),
        ),
        limit=56_000_000,
    )
    act = call(
        functools.partial(act_kernel, plan),
        "act",
        shape((plan.act_rows, 2 * c), BF16),
        (x, cot, timesteps.reshape(1, 1), pay),
        2,
        limit=56_000_000,
    )
    pays = team_gather(act)
    slots = {0: pay, d // 2: to_dom(pay, d // 2)}
    if d > 2:
        slots[d // 4] = to_dom(pay, d // 4)
    slots[d // 2] = call(
        relay_kernel,
        "relay",
        shape((plan.first_rows + plan.second_rows, plan.packed), BF16),
        (slots[d // 2], *([slots[d // 4]] if d > 2 else [])),
        20,
    )
    kinds, half = min(team, 2), -(-team // 2)
    _, chunk, used, _ = fold_layout(plan)
    time_own = call(
        functools.partial(time_kernel, plan),
        "time_own",
        shape((plan.embed // c, plan.wide, c), BF16),
        (time_weight.T,),
        5,
    )
    bit = d // 4
    while bit:
        for slot, value in list(slots.items()):
            if slot + bit not in slots:
                slots[slot + bit] = to_dom(value, bit)
        bit //= 2
    slices = [slots[slot] for slot in range(d)]
    rows = (height + 2) * width
    both = (plan.first_rows + plan.second_rows, plan.packed)
    act2p, w2, *pieces = call(
        functools.partial(main_kernel, plan),
        "main",
        (
            shape((team, rows, plan.wide), BF16),
            shape((3 * plan.wide, c), BF16),
            *[shape(both, BF16 if slot else F32) for slot in range(d)],
        ),
        (owner_map, *pays, *slices, time_own),
        6,
        n_smem=1,
        scratch=(
            pltpu.VMEM((team * pix, 2 * c), BF16),
            pltpu.VMEM((d, local, r), F32),
            pltpu.VMEM((d, plan.piece_pad, c), F32),
            pltpu.VMEM((d, *both), F32),
        ),
    )

    keep, away = call(
        functools.partial(share_kernel, plan),
        "share",
        (shape((half, pix, c), F32), shape((half, pix, c), BF16)),
        (act2p, w2, pieces[0]),
        0.001,
    )
    shares = [keep]
    if team > 1:
        pairs = call(
            pair_kernel,
            "pair",
            tuple(shape((pix, c), BF16 if k else F32) for k in range(half)),
            (keep, to_rep(away, 1)),
            0.001,
        )
        shares = [pairs[0]] + [to_rep(pairs[k], 2 * k) for k in range(1, half)]

    tables = call(
        functools.partial(table_kernel, plan),
        "tables",
        (
            shape((kinds, c, half * plan.first_rows), BF16),
            shape((kinds, c, half * chunk * used), BF16),
            shape((kinds, plan.packed // c * half * plan.second_rows, r), BF16),
        ),
        (shares[0],),
        0.001,
    )

    parts = [pieces[0]] + [to_dom(pieces[step], step) for step in range(1, d)]
    total = call(
        functools.partial(total_kernel, d),
        "total",
        shape(both, BF16 if n_rep == team else F32),
        (*parts, *shares[1:], tables[0]),
        0.001,
    )

    scale = 1.0 / (n_rep * n_dom)
    same_spot = [[i * team + k for i in range(n_rep // team)] for k in range(team)]
    if n_rep > team:
        total = lax.psum(total, "rep", axis_index_groups=same_spot).astype(BF16)
    stack, came = total[None], []
    if team > 1:
        slots = [total] + [to_rep(total, step) for step in range(2, team, 2)]
        stack = call(stack_kernel, "stack", shape((half, *both), BF16), slots, 0.001)
        came = [to_rep(stack, 1)]
    part1, part2 = call(
        functools.partial(part_kernel, plan),
        "part",
        (shape((c, r), F32), shape((c, r), F32)),
        (stack, *tables),
        0.001,
    )
    first, second, output = call(
        functools.partial(last_kernel, plan, scale, len(came)),
        "last",
        (shape((c, r), F32), shape((c, r), F32), shape((pix, c), BF16)),
        (*came, *tables, part1, part2, x, *shares),
        0.1,
        scratch=(
            pltpu.VMEM((c, r), F32),
            pltpu.VMEM((c, r), F32),
            pltpu.VMEM((pix, c), BF16),
            pltpu.SemaphoreType.DMA((3,)),
        ),
        out_hbm=3,
    )
    return output.reshape(1, height, width, c), first.T, second.T


def solution(mesh):
    placed = (
        P(("rep", "dom"), None, None, None),
        P(("rep", "dom"), None, None, None),
        P(("rep", "dom")),
        P(),
        P(),
        P("dom", None),
        P("dom", None),
    )
    return jax.shard_map(
        body,
        mesh=mesh,
        in_specs=placed,
        out_specs=(P(("rep", "dom"), None, None, None), P("dom", None), P("dom", None)),
        check_vma=False,
    )
```

```python
import functools
import math

import jax
import jax.numpy as jnp
from jax import lax
from jax.experimental import pallas as pl
from jax.experimental.pallas import tpu as pltpu
from jax.sharding import PartitionSpec as P

GROUPS = 32
NORM_EPS = 1e-05
F32 = jnp.float32
BF16 = jnp.bfloat16


def round_up(value, unit):
    return -(-value // unit) * unit


def nn(a, b):
    return lax.dot_general(a, b, (((1,), (0,)), ((), ())), preferred_element_type=F32)


def nt(a, b):
    return lax.dot_general(a, b, (((1,), (1,)), ((), ())), preferred_element_type=F32)


def tn(a, b):
    return lax.dot_general(a, b, (((0,), (0,)), ((), ())), preferred_element_type=F32)


def iota(shape, axis):
    return lax.broadcasted_iota(jnp.int32, shape, axis)


def quotient(value, unit):
    return jnp.floor((value.astype(F32) + 0.5) * (1.0 / unit)).astype(jnp.int32)


def one_hot(hit):
    return jnp.where(hit, 1.0, 0.0).astype(BF16)


def silu(value):
    return value / (1.0 + jnp.exp(-value))


class Plan:
    def __init__(self, n_rep, n_dom, height, width, channels, embed, block_rows):
        if n_dom < 2 or n_dom & (n_dom - 1):
            raise ValueError("dom size")
        self.n_rep, self.n_dom = n_rep, n_dom
        self.height, self.width, self.channels = height, width, channels
        self.embed, self.block_rows = embed, block_rows
        self.pixels = height * width
        self.per_group = channels // GROUPS
        team = 1
        while (
            n_rep % (2 * team) == 0
            and GROUPS % (2 * team) == 0
            and block_rows % (2 * team * self.per_group) == 0
        ):
            team *= 2
        self.team = team
        self.local = channels // team
        self.stretch = self.per_group * team
        self.stretches = block_rows // self.stretch
        self.quarters = channels // self.stretch
        self.piece = self.stretches * self.per_group
        self.piece_pad = round_up(self.piece, 16)
        self.wide = round_up(3 * self.local, 128)
        self.act_rows = self.pixels + 16
        self.head = channels // 128 * 128
        self.packed = 2 * channels
        more = block_rows - self.packed
        if more > 0:
            self.first_rows = self.local + folded_rows(self, self.local, more)
        else:
            self.first_rows = folded_rows(self, self.local, block_rows)
        self.first_rows = round_up(self.first_rows, 16)
        self.second_rows = round_up(folded_rows(self, self.piece_pad, channels), 16)


def own_spot(plan):
    return lax.rem(lax.axis_index("rep"), plan.team)


def logical_of(plan, owner_ref, holder):
    total = 0
    for block in range(plan.n_dom):
        total = total + jnp.where(owner_ref[block] == holder, block, 0)
    return total


def group_matrix(plan, lanes, channels):
    row, col = iota((lanes, lanes), 0), iota((lanes, lanes), 1)
    same = quotient(row, plan.per_group) == quotient(col, plan.per_group)
    return one_hot(same & (row < channels) & (col < channels))


def group_sum(sums, same):
    rows = sums.shape[0]
    if rows < 8:
        sums = jnp.concatenate([sums, jnp.zeros((8 - rows, sums.shape[1]), F32)], axis=0)
    high = sums.astype(BF16).astype(F32)
    mid = (sums - high).astype(BF16).astype(F32)
    parts = jnp.concatenate([high, mid, sums - high - mid, jnp.zeros_like(high)], axis=0)
    total = nn(parts.astype(BF16), same)
    return (total[0:8] + total[8:16] + total[16:24])[0:rows]


def fold(plan, value):
    rows, lanes = value.shape
    fits = plan.packed // lanes
    chunk = round_up(-(-rows // fits), 8)
    if chunk * fits > rows:
        value = jnp.concatenate([value, jnp.zeros((chunk * fits - rows, lanes), F32)], axis=0)
    parts = [value[i * chunk : (i + 1) * chunk] for i in range(fits)]
    if fits * lanes < plan.packed:
        parts.append(jnp.zeros((chunk, plan.packed - fits * lanes), F32))
    return parts[0] if len(parts) == 1 else jnp.concatenate(parts, axis=1)


def unfold(plan, value, rows, lanes):
    fits = plan.packed // lanes
    parts = [value[:, i * lanes : (i + 1) * lanes] for i in range(fits)]
    return jnp.concatenate(parts, axis=0)[0:rows]


def folded_rows(plan, rows, lanes):
    return round_up(-(-rows // (plan.packed // lanes)), 8)


def pack_first(plan, value):
    if plan.block_rows > plan.packed:
        parts = [value[:, 0 : plan.packed], fold(plan, value[:, plan.packed :])]
    else:
        parts = [fold(plan, value)]
    have = sum(part.shape[0] for part in parts)
    if have < plan.first_rows:
        parts.append(jnp.zeros((plan.first_rows - have, plan.packed), F32))
    return jnp.concatenate(parts, axis=0) if len(parts) > 1 else parts[0]


def unpack_first(plan, value):
    local, r = plan.local, plan.block_rows
    if r > plan.packed:
        more = r - plan.packed
        tail = unfold(plan, value[local : local + folded_rows(plan, local, more)], local, more)
        return jnp.concatenate([value[0:local], tail], axis=1)
    return unfold(plan, value[0 : folded_rows(plan, local, r)], local, r)


def pack_second(plan, value):
    value = fold(plan, value)
    if value.shape[0] < plan.second_rows:
        rest = jnp.zeros((plan.second_rows - value.shape[0], plan.packed), F32)
        value = jnp.concatenate([value, rest], axis=0)
    return value


def unpack_second(plan, value):
    rows = folded_rows(plan, plan.piece_pad, plan.channels)
    return unfold(plan, value[0:rows], plan.piece_pad, plan.channels)


def local_to_global(plan, index, spot):
    band = quotient(index, plan.per_group)
    return band * plan.stretch + spot * plan.per_group + index - band * plan.per_group


def slice_kernel(plan, w1_any, w2_any, pay_ref, w1_ref, w2_ref, sems):
    copies = [
        pltpu.make_async_copy(src, dst, sems.at[i])
        for i, (src, dst) in enumerate(((w1_any, w1_ref), (w2_any, w2_ref)))
    ]
    for copy in copies:
        copy.start()
    spot = own_spot(plan)
    row, col = iota((plan.local, plan.channels), 0), iota((plan.local, plan.channels), 1)
    pick1 = one_hot(col == local_to_global(plan, row, spot))
    lanes = round_up(plan.piece_pad, 128)
    row, col = iota((plan.block_rows, lanes), 0), iota((plan.block_rows, lanes), 1)
    pick2 = one_hot((row == local_to_global(plan, col, spot)) & (col < plan.piece))
    copies[0].wait()
    pay_ref[0 : plan.first_rows, :] = pack_first(plan, nn(pick1, w1_ref[...])).astype(BF16)
    copies[1].wait()
    pay_ref[plan.first_rows : plan.first_rows + plan.second_rows, :] = pack_second(plan, nn(w2_ref[...], pick2).T[0 : plan.piece_pad]).astype(BF16)


def act_kernel(plan, x_ref, cot_ref, steps_ref, after_ref, act_ref):
    del after_ref
    c, pix, head = plan.channels, plan.pixels, plan.head
    same = group_matrix(plan, c, c)
    count = pix * plan.per_group
    x = x_ref[...].astype(F32)
    off = x - group_sum(jnp.sum(x, 0, keepdims=True), same) / count
    spread = group_sum(jnp.sum(off * off, 0, keepdims=True), same) / count
    act = silu(off * lax.rsqrt(spread + NORM_EPS)).astype(BF16)
    act_ref[0:pix, 0:head] = act[:, 0:head]
    act_ref[0:pix, head : 2 * head] = cot_ref[:, 0:head]
    act_ref[0:pix, 2 * head :] = jnp.concatenate(
        [act[:, head:].astype(F32), cot_ref[:, head:].astype(F32)], axis=1
    ).astype(BF16)
    half = plan.embed // 2
    k = iota((16, c), 0) * c + iota((16, c), 1)
    angle = jnp.where(k < half, k, k - half).astype(F32)
    angle = steps_ref[...].astype(F32) * jnp.exp(-math.log(10000.0) * angle / half)
    wave = silu(jnp.where(k < half, jnp.cos(angle), jnp.sin(angle)))
    wave = jnp.where(iota((16, c), 0) < plan.embed // c, wave, 0.0)
    act_ref[pix:, :] = jnp.concatenate([wave, jnp.zeros((16, c), F32)], axis=1).astype(BF16)


def relay_kernel(pass_ref, *refs):
    refs[-1][...] = pass_ref[0 : refs[-1].shape[0], :]


def time_kernel(plan, tw_ref, out_ref):
    c = plan.channels
    spot = own_spot(plan)
    row, col = iota((plan.wide, c), 0), iota((plan.wide, c), 1)
    pick = one_hot((row < plan.local) & (col == local_to_global(plan, row, spot)))
    own = nn(pick, tw_ref[...])
    for part in range(plan.embed // c):
        out_ref[part] = own[:, part * c : (part + 1) * c].astype(BF16)


def table_kernel(plan, after_ref, main_ref, fold_ref, second_ref):
    del after_ref
    c, spot = plan.channels, own_spot(plan)
    n = -(-plan.team // 2)
    base, chunk, used, _ = fold_layout(plan)
    for kind in range(main_ref.shape[0]):

        def holder(place):
            return (2 * place + kind) ^ spot

        row, col = iota(main_ref.shape[1:], 0), iota(main_ref.shape[1:], 1)
        place = quotient(col, plan.first_rows)
        inner = col - place * plan.first_rows
        hit = (inner < plan.local) & (row == local_to_global(plan, inner, holder(place)))
        main_ref[kind] = one_hot(hit)
        row, col = iota(fold_ref.shape[1:], 0), iota(fold_ref.shape[1:], 1)
        piece = quotient(col, n * chunk)
        place = quotient(col - piece * (n * chunk), chunk)
        inner = col - (piece * n + place - piece) * chunk
        hit = (inner < plan.local) & (row == local_to_global(plan, inner, holder(place)))
        fold_ref[kind] = one_hot(hit)
        row, col = iota(second_ref.shape[1:], 0), iota(second_ref.shape[1:], 1)
        piece = quotient(row, n * plan.second_rows)
        place = quotient(row - piece * (n * plan.second_rows), plan.second_rows)
        inner = row - (piece * n + place) * plan.second_rows
        rows = folded_rows(plan, plan.piece_pad, c)
        hit = (inner < rows) & (inner + piece * rows < plan.piece)
        hit = hit & (col == local_to_global(plan, inner + piece * rows, holder(place)))
        second_ref[kind] = one_hot(hit)


def roll_rows(value, shift, width, plan):
    rows = value.shape[0]
    moved = pltpu.roll(value, shift % rows, 0)
    x = iota(value.shape, 0) & (width - 1) if width & (width - 1) == 0 else lax.rem(iota(value.shape, 0), width)
    return jnp.where(x == (0 if shift == 1 else width - 1), 0.0, moved)


def roll_lanes(value, shift):
    lanes = value.shape[1]
    return value if shift % lanes == 0 else pltpu.roll(value, shift % lanes, 1)


def gather_taps(wide, plan, sign):
    left = roll_rows(wide, sign, plan.width, plan)
    right = roll_rows(roll_lanes(wide, -2 * plan.local), -sign, plan.width, plan)
    return left + roll_lanes(wide, -plan.local) + right


def spread_taps(value, plan, sign):
    left = roll_rows(value, sign, plan.width, plan)
    right = roll_rows(value, -sign, plan.width, plan)
    return left + roll_lanes(value, plan.local) + roll_lanes(right, 2 * plan.local)


def window(plan, pad, tap):
    value = pad[:, tap * plan.width : tap * plan.width + plan.pixels, :]
    return value.reshape(value.shape[0] * plan.pixels, value.shape[2])


def fill_pad(plan, pad):
    pad[:, 0 : plan.width, :] = jnp.zeros((pad.shape[0], plan.width, pad.shape[2]), BF16)
    pad[:, plan.width + plan.pixels :, :] = jnp.zeros((pad.shape[0], plan.width, pad.shape[2]), BF16)


def group_mean(plan, value, same):
    team, wide = plan.team, plan.wide
    sums = jnp.sum(value.reshape(team, plan.pixels, wide), axis=1)
    sums = [group_sum(sums[k : k + 8], same) for k in range(0, team, 8)]
    sums = sums[0] if len(sums) == 1 else jnp.concatenate(sums, axis=0)
    return sums.reshape(team, 1, wide) * (1.0 / (plan.pixels * plan.per_group))


def row_taps(plan, value, sign):
    team, pix, wide, width = plan.team, plan.pixels, plan.wide, plan.width
    value = value.reshape(team, pix, 3 * wide)
    edge = jnp.zeros((team, width, wide), F32)
    low, mid, high = (value[:, :, k * wide : (k + 1) * wide] for k in range(3))
    if sign < 0:
        low, high = high, low
    low = jnp.concatenate([edge, low[:, : pix - width]], axis=1)
    high = jnp.concatenate([high[:, width:], edge], axis=1)
    return (low + mid + high).reshape(team * pix, wide)


def stack_rows(plan, value, sign):
    width, pix = plan.width, plan.pixels
    lanes = value.shape[1]
    inside = lax.rem(iota(value.shape, 1), pix)
    above = jnp.where(inside < width, 0.0, pltpu.roll(value, width, 1))
    below = jnp.where(inside >= pix - width, 0.0, pltpu.roll(value, lanes - width, 1))
    order = (above, value, below) if sign > 0 else (below, value, above)
    return jnp.concatenate([part.astype(BF16) for part in order], axis=0)


def main_kernel(plan, owner_ref, *refs):
    team, d, c, pix, local, wide = plan.team, plan.n_dom, plan.channels, plan.pixels, plan.local, plan.wide
    pays, slices, tw_ref = refs[0:team], refs[team : team + d], refs[team + d]
    act2p, w2_ref = refs[team + d + 1 : team + d + 3]
    pieces = refs[team + d + 3 : team + 2 * d + 3]
    maps, w1st, w2st, held = refs[team + 2 * d + 3 :]
    here = lax.axis_index("dom")
    rows, width, head = team * pix, plan.width, plan.head
    tail = c - head

    for slot in range(team):
        maps[slot * pix : (slot + 1) * pix, :] = pays[slot][0:pix, :]

    for slot in range(d):
        block = logical_of(plan, owner_ref, here ^ slot)
        w1st[block] = unpack_first(plan, slices[slot][0 : plan.first_rows, :].astype(F32))
        w2st[block] = unpack_second(plan, slices[slot][plan.first_rows : plan.first_rows + plan.second_rows, :].astype(F32))
    flat = jnp.concatenate([w1st[b] for b in range(d)], axis=1)
    zeros = [jnp.zeros((wide - 3 * local, c), F32)] if wide > 3 * local else []
    w1 = []
    for ky in range(3):
        w1 += [flat[:, t * c : (t + 1) * c] for t in range(3 * ky, 3 * ky + 3)] + zeros
    w1 = jnp.concatenate(w1, axis=0)
    flat = jnp.concatenate([w2st[b][0 : plan.piece] for b in range(d)], axis=0)
    w2 = []
    for ky in range(3):
        w2 += [flat[3 * local * ky : 3 * local * (ky + 1)]] + zeros
    w2 = jnp.concatenate(w2, axis=0)
    w2_ref[...] = w2.astype(BF16)

    lane_ok = iota((1, wide), 1) < local
    same = group_matrix(plan, wide, local)
    none = jnp.zeros((3 * wide, tail), F32)
    w1_tail = jnp.concatenate([w1[:, head:], none], axis=1).astype(BF16)
    w2_tail = jnp.concatenate([none, w2[:, head:]], axis=1).astype(BF16)
    conv = nt(maps[:, 0:head], w1[:, 0:head].astype(BF16)) + nt(maps[:, 2 * head :], w1_tail)
    conv = gather_taps(row_taps(plan, conv, 1), plan, 1)
    tails = jnp.concatenate([pays[slot][pix:, 0:c] for slot in range(team)], axis=0)
    row = iota((16, wide), 0)
    bias = jnp.zeros((team, 16, wide), F32)
    for part in range(plan.embed // c):
        product = nt(tails, tw_ref[part]).reshape(team, 16, wide)
        bias = bias + jnp.where(row == part, product, 0.0)
    bias = jnp.sum(bias, axis=1, keepdims=True)
    conv = jnp.where(lane_ok, conv, 0.0).reshape(team, pix, wide) + bias
    off = conv - group_mean(plan, conv.reshape(rows, wide), same)
    inverse = lax.rsqrt(group_mean(plan, (off * off).reshape(rows, wide), same) + NORM_EPS)
    norm = (off * inverse).reshape(rows, wide)
    gate = 1.0 / (1.0 + jnp.exp(-norm))
    act2x = spread_taps(norm * gate, plan, 1)
    fill_pad(plan, act2p)
    act2p[:, width : width + pix, :] = act2x.astype(BF16).reshape(team, pix, wide)

    back = nt(maps[:, head : 2 * head], w2[:, 0:head].astype(BF16)) + nt(maps[:, 2 * head :], w2_tail)
    back = jnp.where(lane_ok, gather_taps(row_taps(plan, back, -1), plan, -1), 0.0)
    grad = back * gate * (1.0 + norm * (1.0 - gate))
    grad_mean = group_mean(plan, grad, same)
    prod_mean = group_mean(plan, grad * norm, same)
    shaped = (team, pix, wide)
    grad = inverse * (grad.reshape(shaped) - grad_mean - norm.reshape(shaped) * prod_mean)
    grad = jnp.where(lane_ok, grad, 0.0).reshape(rows, wide).astype(BF16).astype(F32)

    act2t = stack_rows(plan, act2x.T, 1)
    gradt = stack_rows(plan, spread_taps(grad, plan, -1).T, -1)
    tails = nn(jnp.concatenate([gradt, act2t], axis=0), maps[:, 2 * head :])
    first = jnp.concatenate([nn(gradt, maps[:, 0:head]), tails[0 : 3 * wide, 0:tail]], axis=1)
    second = jnp.concatenate([nn(act2t, maps[:, head : 2 * head]), tails[3 * wide :, tail:]], axis=1)
    flat = []
    for t in range(9):
        start = t // 3 * wide + t % 3 * local
        flat.append(first[start : start + local])
    flat = jnp.concatenate(flat, axis=1)
    for block in range(d):
        value = flat[:, block * plan.block_rows : (block + 1) * plan.block_rows]
        held[block, 0 : plan.first_rows, :] = pack_first(plan, value)
    flat = [second[ky * wide : ky * wide + 3 * local] for ky in range(3)]
    rest = jnp.zeros((plan.piece_pad - plan.piece, c), F32)
    flat = jnp.concatenate([*flat, rest] if rest.shape[0] else flat, axis=0)
    for block in range(d):
        value = flat[block * plan.piece : block * plan.piece + plan.piece_pad]
        held[block, plan.first_rows :, :] = pack_second(plan, value)
    for slot in range(d):
        piece = held[logical_of(plan, owner_ref, here ^ slot)]
        pieces[slot][...] = piece.astype(pieces[slot].dtype)


def share_kernel(plan, act2p, w2_ref, after_ref, keep_ref, away_ref):
    del after_ref
    team, c, pix = plan.team, plan.channels, plan.pixels
    out = nn(jnp.concatenate([window(plan, act2p, ky) for ky in range(3)], axis=1), w2_ref[...])
    out = out.reshape(team, pix, c)
    for slot in range(team):
        if slot % 2:
            away_ref[slot // 2] = out[slot].astype(BF16)
        else:
            keep_ref[slot // 2] = out[slot]


def pair_kernel(keep_ref, came_ref, *outs):
    for k, out in enumerate(outs):
        out[...] = (keep_ref[k] + came_ref[k].astype(F32)).astype(out.dtype)


def total_kernel(n, *refs):
    total = refs[0][...].astype(F32)
    for ref in refs[1:n]:
        total = total + ref[...].astype(F32)
    refs[-1][...] = total.astype(refs[-1].dtype)


def stack_kernel(*refs):
    for k, ref in enumerate(refs[:-1]):
        refs[-1][k] = ref[...]


def fold_layout(plan):
    more = plan.block_rows - plan.packed
    base, lanes = (plan.local, more) if more > 0 else (0, plan.block_rows)
    chunk = folded_rows(plan, plan.local, lanes)
    return base, chunk, -(-plan.local // chunk), lanes


def first_in_place(plan, stack_ref, main_table, fold_table):
    n = stack_ref.shape[0]
    base, chunk, used, lanes = fold_layout(plan)
    low = base // 16 * 16
    folded = stack_ref[:, low : round_up(base + chunk, 16), :].astype(F32)
    folded = folded[:, base - low : base - low + chunk].reshape(n * chunk, plan.packed)
    folded = [folded[:, k * lanes : (k + 1) * lanes] for k in range(used)]
    first = nn(fold_table, jnp.concatenate(folded, axis=0).astype(BF16))
    if not base:
        return first
    rows = stack_ref[:, 0 : plan.first_rows, :].reshape(n * plan.first_rows, plan.packed)
    return jnp.concatenate([nn(main_table, rows), first], axis=1)


def second_in_place(plan, stack_ref, table):
    n, c = stack_ref.shape[0], plan.channels
    rows = stack_ref[:, plan.first_rows :, :].reshape(n * plan.second_rows, plan.packed)
    rows = [rows[:, k * c : (k + 1) * c] for k in range(plan.packed // c)]
    return tn(jnp.concatenate(rows, axis=0), table)


def part_kernel(plan, stack_ref, main_ref, fold_ref, second_ref, x_ref, *refs):
    *shares, out1_ref, out2_ref, output_ref = refs
    total = x_ref[...].astype(F32)
    for ref in shares:
        total = total + ref[...].reshape(total.shape).astype(F32)
    output_ref[...] = total.astype(BF16)
    out1_ref[...] = first_in_place(plan, stack_ref, main_ref[0], fold_ref[0])
    out2_ref[...] = second_in_place(plan, stack_ref, second_ref[0])


def last_kernel(plan, scale, n_came, *refs):
    came, tables, part1_ref, part2_ref = refs[0:n_came], refs[n_came : n_came + 3], *refs[n_came + 3 : n_came + 5]
    first_any, second_any, first_ref, second_ref, sems = refs[-5:]
    first = part1_ref[...]
    for ref in came:
        first = first + first_in_place(plan, ref, tables[0][1], tables[1][1])
    first_ref[...] = first * scale
    copy1 = pltpu.make_async_copy(first_ref, first_any, sems.at[0])
    copy1.start()
    second = part2_ref[...]
    for ref in came:
        second = second + second_in_place(plan, ref, tables[2][1])
    second_ref[...] = second * scale
    copy2 = pltpu.make_async_copy(second_ref, second_any, sems.at[1])
    copy2.start()
    copy1.wait()
    copy2.wait()


VMEM = pl.BlockSpec(memory_space=pltpu.VMEM)
SMEM = pl.BlockSpec(memory_space=pltpu.SMEM)


HBM = pl.BlockSpec(memory_space=pltpu.HBM)


def call(kernel, name, out_shape, operands, cost, n_smem=0, n_hbm=0, scratch=(), limit=48 * 1024 * 1024, out_hbm=0):
    n = len(operands)
    return pl.pallas_call(
        kernel,
        name=name,
        out_shape=out_shape,
        in_specs=[SMEM] * n_smem + [HBM] * n_hbm + [VMEM] * (n - n_smem - n_hbm),
        out_specs=[HBM] * out_hbm + [VMEM] * (len(out_shape) - out_hbm) if isinstance(out_shape, tuple) else VMEM,
        scratch_shapes=list(scratch),
        compiler_params=pltpu.CompilerParams(vmem_limit_bytes=limit),
        cost_estimate=pl.CostEstimate(
            flops=int(cost * 1e9), bytes_accessed=int(cost * 3e6), transcendentals=0
        ),
    )(*operands)


def shape(dims, dtype):
    return jax.ShapeDtypeStruct(dims, dtype)


def body(block_input, cotangent, timesteps, owner_map, time_weight, first_weight, second_weight):
    n_rep, n_dom = lax.axis_size("rep"), lax.axis_size("dom")
    height, width, c = block_input.shape[1:]
    plan = Plan(n_rep, n_dom, height, width, c, time_weight.shape[0], first_weight.shape[0])
    team, d, pix = plan.team, n_dom, plan.pixels
    r, local = plan.block_rows, plan.local
    def to_rep(value, step):
        return lax.ppermute(value, "rep", [(i, i ^ step) for i in range(n_rep)])

    def to_dom(value, step):
        return lax.ppermute(value, "dom", [(i, i ^ step) for i in range(d)])

    def team_gather(value):
        slots = [value] + [None] * (team - 1)
        for step in range(2, team, 2):
            slots[step] = to_rep(value, step)
        if team > 1:
            for step in range(0, team, 2):
                slots[step + 1] = to_rep(slots[step], 1)
        return slots

    x = block_input.reshape(pix, c)
    cot = cotangent.reshape(pix, c)
    pay = call(
        functools.partial(slice_kernel, plan),
        "slices",
        shape((plan.first_rows + plan.second_rows + 0, plan.packed), BF16),
        (first_weight.T, second_weight.T),
        2,
        n_hbm=2,
        scratch=(
            pltpu.VMEM((c, r), BF16),
            pltpu.VMEM((c, r), BF16),
            pltpu.SemaphoreType.DMA((2,)),
        ),
        limit=56_000_000,
    )
    act = call(
        functools.partial(act_kernel, plan),
        "act",
        shape((plan.act_rows, 2 * c), BF16),
        (x, cot, timesteps.reshape(1, 1), pay),
        2,
        limit=56_000_000,
    )
    pays = team_gather(act)
    slots = {0: pay, d // 2: to_dom(pay, d // 2)}
    if d > 2:
        slots[d // 4] = to_dom(pay, d // 4)
    slots[d // 2] = call(
        relay_kernel,
        "relay",
        shape((plan.first_rows + plan.second_rows, plan.packed), BF16),
        (slots[d // 2], *([slots[d // 4]] if d > 2 else [])),
        20,
    )
    kinds, half = min(team, 2), -(-team // 2)
    _, chunk, used, _ = fold_layout(plan)
    time_own = call(
        functools.partial(time_kernel, plan),
        "time_own",
        shape((plan.embed // c, plan.wide, c), BF16),
        (time_weight.T,),
        5,
    )
    bit = d // 4
    while bit:
        for slot, value in list(slots.items()):
            if slot + bit not in slots:
                slots[slot + bit] = to_dom(value, bit)
        bit //= 2
    slices = [slots[slot] for slot in range(d)]
    rows = (height + 2) * width
    both = (plan.first_rows + plan.second_rows, plan.packed)
    act2p, w2, *pieces = call(
        functools.partial(main_kernel, plan),
        "main",
        (
            shape((team, rows, plan.wide), BF16),
            shape((3 * plan.wide, c), BF16),
            *[shape(both, BF16 if slot else F32) for slot in range(d)],
        ),
        (owner_map, *pays, *slices, time_own),
        6,
        n_smem=1,
        scratch=(
            pltpu.VMEM((team * pix, 2 * c), BF16),
            pltpu.VMEM((d, local, r), F32),
            pltpu.VMEM((d, plan.piece_pad, c), F32),
            pltpu.VMEM((d, *both), F32),
        ),
    )

    keep, away = call(
        functools.partial(share_kernel, plan),
        "share",
        (shape((half, pix, c), F32), shape((half, pix, c), BF16)),
        (act2p, w2, pieces[0]),
        0.001,
    )
    shares = [keep]
    if team > 1:
        pairs = call(
            pair_kernel,
            "pair",
            tuple(shape((pix, c), BF16 if k else F32) for k in range(half)),
            (keep, to_rep(away, 1)),
            0.001,
        )
        shares = [pairs[0]] + [to_rep(pairs[k], 2 * k) for k in range(1, half)]

    tables = call(
        functools.partial(table_kernel, plan),
        "tables",
        (
            shape((kinds, c, half * plan.first_rows), BF16),
            shape((kinds, c, half * chunk * used), BF16),
            shape((kinds, plan.packed // c * half * plan.second_rows, r), BF16),
        ),
        (shares[0],),
        0.001,
    )

    parts = [pieces[0]] + [to_dom(pieces[step], step) for step in range(1, d)]
    total = call(
        functools.partial(total_kernel, d),
        "total",
        shape(both, BF16 if n_rep == team else F32),
        (*parts, *shares[1:], tables[0]),
        0.001,
    )

    scale = 1.0 / (n_rep * n_dom)
    same_spot = [[i * team + k for i in range(n_rep // team)] for k in range(team)]
    if n_rep > team:
        total = lax.psum(total, "rep", axis_index_groups=same_spot).astype(BF16)
    stack, came = total[None], []
    if team > 1:
        slots = [total] + [to_rep(total, step) for step in range(2, team, 2)]
        stack = call(stack_kernel, "stack", shape((half, *both), BF16), slots, 0.001)
        came = [to_rep(stack, 1)]
    part1, part2, output = call(
        functools.partial(part_kernel, plan),
        "part",
        (shape((c, r), F32), shape((c, r), F32), shape((pix, c), BF16)),
        (stack, *tables, x, *shares),
        0.001,
    )
    first, second = call(
        functools.partial(last_kernel, plan, scale, len(came)),
        "last",
        (shape((c, r), F32), shape((c, r), F32)),
        (*came, *tables, part1, part2),
        0.1,
        scratch=(
            pltpu.VMEM((c, r), F32),
            pltpu.VMEM((c, r), F32),
            pltpu.SemaphoreType.DMA((2,)),
        ),
        out_hbm=2,
    )
    return output.reshape(1, height, width, c), first.T, second.T


def solution(mesh):
    placed = (
        P(("rep", "dom"), None, None, None),
        P(("rep", "dom"), None, None, None),
        P(("rep", "dom")),
        P(),
        P(),
        P("dom", None),
        P("dom", None),
    )
    return jax.shard_map(
        body,
        mesh=mesh,
        in_specs=placed,
        out_specs=(P(("rep", "dom"), None, None, None), P("dom", None), P("dom", None)),
        check_vma=False,
    )
```
